256 devices in a mesh: ex: 16 (over x_hi, y, core), mat: 16 (over x_lo, z).
Axes of the slice: x: 4 (x_hi: 2, x_lo: 2; x = x_hi * 2 + x_lo), y: 4, z: 8, core: 2. Of those that a mesh axis runs over, the one named last changes fastest.
Arguments:
- train_grads: bfloat16 [16384, 16, 2048], P(('ex', 'mat')), may hold values from -6 to 6
- inverse_hessian: bfloat16 [16, 2048, 2048], P('mat'), as said below
- query_grads: bfloat16 [256, 16, 2048], P('ex', 'mat'), may hold values from -0.046875 to 0.046875
Outputs:
- preconditioned: bfloat16 [16384, 16, 2048], P('ex', 'mat')
- scores: float32 [256, 16384], P('mat', 'ex')
The draws below stay inside these ranges and needn't reach their ends.
Inputs may be any that keep to these rules, and one draw needn't show every extreme that they name: `inverse_hessian`: each matrix is its diagonal plus full-rank terms off it.
All inputs are finite; a program needn't handle non-finite values.
Results may differ from the reference program's by a relative error of at most 0.0029.
Values may be sent and summed in bfloat16 or wider, within the bound.
A program may use at most 128 MiB of HBM per device.

```python
import jax
import jax.numpy as jnp
from jax import lax

K = 2048
M = 16
N = 16384
QN = 256


def draw_inverse_hessian(key, part):
    key_diag = jax.random.fold_in(key, 11)
    key_off = jax.random.fold_in(key, 23)
    logs = jax.random.uniform(key_diag, (M, K), jnp.float32, jnp.log(0.3), jnp.log(3.0))
    diagonal = jnp.exp(logs)
    noise = jax.random.normal(key_off, (M, K, K), jnp.float32)
    identity = jnp.eye(K, dtype=jnp.float32)
    matrix = diagonal[:, :, None] * identity[None, :, :] + noise * (0.6 / K ** 0.5)
    return matrix.astype(jnp.bfloat16)


def with_spikes(array, stream_key, source, target, parts, factor):
    def block_of(dim):
        return (jnp.arange(array.shape[dim]) // (array.shape[dim] // parts)).reshape((-1,) + (1,) * (array.ndim - 1 - dim))

    near = jax.random.permutation(stream_key, parts)[block_of(target)]
    second = (block_of(target) + parts // 2) % parts
    return jnp.where((block_of(source) == near) | (block_of(source) == second), factor * array, array)


def block_scale(key, extent, cuts, smallest, high):
    factor_of = 1.0
    for dim, shards_of in cuts:
        steps = jax.random.uniform(jax.random.fold_in(jax.random.fold_in(key, 6), dim), (shards_of,), jnp.float32, smallest / len(cuts), high / len(cuts))
        factor_of = factor_of * jnp.repeat(jnp.exp(steps), extent[dim] // shards_of).reshape((-1,) + (1,) * (len(extent) - 1 - dim))
    return factor_of


def centred(key, extent, deviation, bound, cuts=(), kind=jnp.bfloat16):
    values = jax.random.normal(key, extent, jnp.float32) * deviation
    if len(cuts) > 0:
        values = block_scale(key, extent, cuts, -0.22, 0.18) * values
    return jnp.clip(values, min=-bound, max=bound).astype(kind)


def bell_draw_with(rng, dims, spread, bound, cuts, heavy, kind=jnp.bfloat16):
    drawn = spread * jax.random.normal(rng, dims, jnp.float32)
    if cuts:
        drawn = drawn * block_scale(rng, dims, cuts, -0.22, 0.18)
    return jnp.clip(with_spikes(drawn, jax.random.fold_in(rng, 3), *heavy), -bound, bound).astype(kind)


def setup_inputs(seed: int = 0) -> dict:
    keys = jax.random.split(jax.random.key(seed), 4)
    train_grads = centred(keys[0], (N, M, K), 1.0, 6.0, ((0, 256),))
    inverse_hessian = draw_inverse_hessian(jax.random.fold_in(keys[3], 71), 0)
    query_grads = bell_draw_with(keys[2], (QN, M, K), (M * K) ** -0.5, 0.046875, ((0, 16), (1, 16)), (1, 0, 16, 2.0))
    return dict(train_grads=train_grads, inverse_hessian=inverse_hessian, query_grads=query_grads)


def reference(train_grads, inverse_hessian, query_grads):
    grads_major = jnp.moveaxis(train_grads, 1, 0)
    query_major = jnp.moveaxis(query_grads, 1, 0)

    def precondition(pair):
        rows, matrix = pair
        product = jnp.dot(rows.astype(jnp.float32), matrix.astype(jnp.float32), preferred_element_type=jnp.float32)
        return product.astype(jnp.bfloat16)

    pre_major = lax.map(precondition, (grads_major, inverse_hessian))

    def accumulate(total, pair):
        queries, rows = pair
        term = jnp.dot(queries.astype(jnp.float32), rows.astype(jnp.float32).T, preferred_element_type=jnp.float32)
        return total + term, None

    start = jnp.zeros((QN, N), jnp.float32)
    scores, unused = lax.scan(accumulate, start, (query_major, pre_major))
    return jnp.moveaxis(pre_major, 0, 1), scores
```

```python
import functools

import jax
import jax.numpy as jnp
from jax import lax
from jax.experimental import pallas as pl
from jax.experimental.pallas import tpu as pltpu
from jax.sharding import PartitionSpec as P

MESH = pl.DeviceIdType.MESH
F32, BF16 = jnp.float32, jnp.bfloat16
GROUPS = 4
ZS = 8
TILE = 512

PEERS = (
    (0, 4), (1, 4), (0, 3), (0, 5), (1, 3), (1, 5), (0, 2), (0, 6),
    (1, 2), (1, 6), (0, 1), (0, 7), (1, 1), (1, 7), (1, 0),
)


def peer(me, offset, sign):
    dx, dz = offset
    x, z = me // ZS, lax.rem(me, ZS)
    return lax.rem(x + dx, 2) * ZS + lax.rem(z + (dz if sign > 0 else ZS - dz), ZS)


def kernel(
    n_ex,
    n_mat,
    train_ref,
    hess_ref,
    query_ref,
    pre_ref,
    scores_ref,
    staged,
    outgoing,
    arrived,
    hess,
    queries,
    pre,
    terms,
    terms_in,
    load_sem,
    hess_sem,
    query_load_sem,
    send_sem,
    recv_sem,
    query_send_sem,
    query_recv_sem,
    term_send_sem,
    term_recv_sem,
    out_sem,
):
    me = lax.axis_index("mat")
    my_ex = lax.axis_index("ex")
    group_rows = train_ref.shape[0] // GROUPS
    part = group_rows // n_mat
    columns = train_ref.shape[1]

    def load(g):
        rows = pl.ds(g * group_rows, group_rows)
        return pltpu.make_async_copy(train_ref.at[rows], staged.at[g], load_sem.at[g])

    my_queries = pl.ds(pl.multiple_of(my_ex * 16, 16), 16)
    query_load = pltpu.make_async_copy(query_ref, queries.at[my_queries], query_load_sem)
    hess_load = pltpu.make_async_copy(hess_ref, hess, hess_sem)

    for g in range(GROUPS):
        load(g).start()
    query_load.start()
    hess_load.start()

    barrier = pltpu.get_barrier_semaphore()
    for k in range(1, n_mat):
        pl.semaphore_signal(
            barrier, inc=1, device_id={"mat": lax.rem(me + k, n_mat)}, device_id_type=MESH
        )
    for k in range(1, n_ex):
        pl.semaphore_signal(
            barrier, inc=1, device_id={"ex": lax.rem(my_ex + k, n_ex)}, device_id_type=MESH
        )

    out_row = lax.broadcasted_iota(jnp.int32, (group_rows, group_rows), 0)
    in_row = lax.broadcasted_iota(jnp.int32, (group_rows, group_rows), 1)
    regroup = jnp.where(
        in_row == lax.rem(out_row, part) * n_mat + out_row // part, 1.0, 0.0
    ).astype(BF16)
    mine = pl.ds(pl.multiple_of(me * part, part), part)

    def regroup_rows(g):
        load(g).wait()
        for c in range(columns // TILE):
            cols = pl.ds(c * TILE, TILE)
            outgoing[g, :, cols] = jnp.dot(
                regroup, staged[g, :, cols], preferred_element_type=F32
            ).astype(BF16)
        arrived[g, mine, :] = outgoing[g, mine, :]

    def send(g, i):
        to = peer(me, PEERS[i], 1)
        return pltpu.make_async_remote_copy(
            src_ref=outgoing.at[g, pl.ds(pl.multiple_of(to * part, part), part)],
            dst_ref=arrived.at[g, mine],
            send_sem=send_sem.at[g, i],
            recv_sem=recv_sem.at[g, i],
            device_id={"mat": to},
            device_id_type=MESH,
        )

    def arrival(g, i):
        source = peer(me, PEERS[i], -1)
        rows = pl.ds(pl.multiple_of(source * part, part), part)
        return pltpu.make_async_remote_copy(
            src_ref=outgoing.at[g, rows],
            dst_ref=arrived.at[g, rows],
            send_sem=send_sem.at[g, i],
            recv_sem=recv_sem.at[g, i],
            device_id={"mat": source},
            device_id_type=MESH,
        )

    def query_send(k):
        return pltpu.make_async_remote_copy(
            src_ref=queries.at[my_queries],
            dst_ref=queries.at[my_queries],
            send_sem=query_send_sem.at[k],
            recv_sem=query_recv_sem.at[k],
            device_id={"ex": lax.rem(my_ex + k, n_ex)},
            device_id_type=MESH,
        )

    def query_arrival(k):
        source = lax.rem(my_ex + n_ex - k, n_ex)
        rows = pl.ds(pl.multiple_of(source * 16, 16), 16)
        return pltpu.make_async_remote_copy(
            src_ref=queries.at[rows],
            dst_ref=queries.at[rows],
            send_sem=query_send_sem.at[k],
            recv_sem=query_recv_sem.at[k],
            device_id={"ex": source},
            device_id_type=MESH,
        )

    def term_send(g, i):
        to = peer(me, PEERS[i], 1)
        return pltpu.make_async_remote_copy(
            src_ref=terms.at[g, pl.ds(pl.multiple_of(to * 16, 16), 16)],
            dst_ref=terms_in.at[g, i + 1],
            send_sem=term_send_sem.at[g, i],
            recv_sem=term_recv_sem.at[g, i],
            device_id={"mat": to},
            device_id_type=MESH,
        )

    def out_copy(g, k):
        rows = pl.ds(pl.multiple_of(k * (part * GROUPS) + g * part, part), part)
        return pltpu.make_async_copy(
            pre.at[g, pl.ds(k * part, part)], pre_ref.at[rows], out_sem.at[g, k]
        )

    regroup_rows(0)
    query_load.wait()
    pl.semaphore_wait(barrier, n_mat + n_ex - 2)
    for i in range(len(PEERS)):
        send(0, i).start()
    for k in range(1, n_ex):
        query_send(k).start()
    regroup_rows(1)
    for i in range(len(PEERS)):
        send(1, i).start()
    for g in range(2, GROUPS):
        regroup_rows(g)

    my_terms = pl.ds(pl.multiple_of(me * 16, 16), 16)
    for g in range(GROUPS):
        for i in range(len(PEERS)):
            arrival(g, i).wait_recv()
        if g + 2 < GROUPS:
            for i in range(len(PEERS)):
                send(g + 2, i).start()
        if g == 0:
            hess_load.wait()

        def multiply(c, carry, g=g):
            cols = pl.ds(pl.multiple_of(c * TILE, TILE), TILE)
            pre[g, :, cols] = jnp.dot(
                arrived[g], hess[:, cols], preferred_element_type=F32
            ).astype(BF16)
            return carry

        lax.fori_loop(0, columns // TILE, multiply, 0)
        for k in range(n_mat):
            out_copy(g, k).start()
        if g == 0:
            for k in range(1, n_ex):
                query_arrival(k).wait_recv()
        terms[g] = lax.dot_general(
            queries[...], pre[g], (((1,), (1,)), ((), ())), preferred_element_type=F32
        ).astype(BF16)
        for i in range(len(PEERS)):
            term_send(g, i).start()
        terms_in[g, 0] = terms[g, my_terms, :]

    lane = lax.broadcasted_iota(jnp.int32, (16, 128), 1)
    totals = []
    for g in range(GROUPS):
        for i in range(len(PEERS)):
            term_send(g, i).wait_recv()
        total = terms_in[g, 0].astype(F32)
        for i in range(len(PEERS)):
            total += terms_in[g, i + 1].astype(F32)
        totals.append(total)
    for j in range(scores_ref.shape[1] // 128):
        tile = jnp.zeros((16, 128), F32)
        for s in range(2):
            source = 2 * j + s
            at, of = (source * part) % 128, source * part // 128
            for g in range(GROUPS):
                to = s * 64 + g * part
                moved = pltpu.roll(totals[g][:, of * 128 : of * 128 + 128], (to - at) % 128, 1)
                tile = jnp.where((lane >= to) & (lane < to + part), moved, tile)
        scores_ref[:, j * 128 : j * 128 + 128] = tile

    for g in range(GROUPS):
        for i in range(len(PEERS)):
            send(g, i).wait_send()
            term_send(g, i).wait_send()
        for k in range(n_mat):
            out_copy(g, k).wait()
    for k in range(1, n_ex):
        query_send(k).wait_send()


def on_device(n_ex, n_mat, train_grads, inverse_hessian, query_grads):
    rows, mats, columns = train_grads.shape
    all_rows = rows * mats
    group_rows = all_rows // GROUPS
    n_queries = query_grads.shape[0] * n_ex
    dma = pltpu.SemaphoreType.DMA
    pre, scores = pl.pallas_call(
        functools.partial(kernel, n_ex, n_mat),
        name="influence",
        out_shape=(
            jax.ShapeDtypeStruct((all_rows, columns), BF16),
            jax.ShapeDtypeStruct((n_queries // n_mat, all_rows), F32),
        ),
        in_specs=[pl.BlockSpec(memory_space=pl.ANY)] * 3,
        out_specs=(
            pl.BlockSpec(memory_space=pl.ANY),
            pl.BlockSpec(memory_space=pltpu.VMEM),
        ),
        scratch_shapes=[
            pltpu.VMEM((GROUPS, group_rows, columns), BF16),
            pltpu.VMEM((GROUPS, group_rows, columns), BF16),
            pltpu.VMEM((GROUPS, group_rows, columns), BF16),
            pltpu.VMEM((columns, columns), BF16),
            pltpu.VMEM((n_queries, columns), BF16),
            pltpu.VMEM((GROUPS, group_rows, columns), BF16),
            pltpu.VMEM((GROUPS, n_queries, group_rows), BF16),
            pltpu.VMEM((GROUPS, n_mat, n_queries // n_mat, group_rows), BF16),
            dma((GROUPS,)),
            dma,
            dma,
            dma((GROUPS, n_mat)),
            dma((GROUPS, n_mat)),
            dma((n_ex,)),
            dma((n_ex,)),
            dma((GROUPS, n_mat)),
            dma((GROUPS, n_mat)),
            dma((GROUPS, n_mat)),
        ],
        compiler_params=pltpu.CompilerParams(
            collective_id=0, has_side_effects=True, vmem_limit_bytes=56 * 2**20
        ),
        cost_estimate=pl.CostEstimate(
            flops=2 * all_rows * columns * (columns + n_queries),
            bytes_accessed=2 * columns * (2 * all_rows + columns),
            transcendentals=0,
        ),
    )(
        train_grads.reshape(all_rows, columns),
        inverse_hessian.reshape(columns, columns),
        query_grads.reshape(query_grads.shape[0], columns),
    )
    return pre.reshape(all_rows, 1, columns), scores


def solution(mesh):
    return jax.shard_map(
        functools.partial(on_device, mesh.shape["ex"], mesh.shape["mat"]),
        mesh=mesh,
        in_specs=(P(("ex", "mat"), None, None), P("mat", None, None), P("ex", "mat", None)),
        out_specs=(P("ex", "mat", None), P("mat", "ex")),
        check_vma=False,
    )
```

```python
import functools

import jax
import jax.numpy as jnp
from jax import lax
from jax.experimental import pallas as pl
from jax.experimental.pallas import tpu as pltpu
from jax.sharding import PartitionSpec as P

MESH = pl.DeviceIdType.MESH
F32, BF16 = jnp.float32, jnp.bfloat16
GROUPS = 4
ZS = 8
TILE = 512
WIDE = 1024
AHEAD = 8
PASS_AT = 11

PEERS = (
    (0, 4), (1, 4), (0, 3), (0, 5), (1, 3), (1, 5), (0, 2), (0, 6),
    (1, 2), (1, 6), (0, 1), (0, 7), (1, 1), (1, 7), (1, 0),
)


def peer(me, offset, sign):
    dx, dz = offset
    x, z = me // ZS, lax.rem(me, ZS)
    return lax.rem(x + dx, 2) * ZS + lax.rem(z + (dz if sign > 0 else ZS - dz), ZS)


def kernel(
    n_ex,
    n_mat,
    train_ref,
    hess_ref,
    query_ref,
    pre_ref,
    scores_ref,
    staged,
    outgoing,
    arrived,
    hess,
    queries,
    carried,
    terms,
    own,
    x_out,
    x_in,
    z_out,
    z_in,
    last_out,
    last_in,
    load_sem,
    hess_sem,
    query_load_sem,
    send_sem,
    recv_sem,
    query_send_sem,
    query_recv_sem,
    x_send_sem,
    x_recv_sem,
    z_send_sem,
    z_recv_sem,
    term_send_sem,
    term_recv_sem,
):
    me = lax.axis_index("mat")
    my_ex = lax.axis_index("ex")
    group_rows = train_ref.shape[0] // GROUPS
    part = group_rows // n_mat
    columns = train_ref.shape[1]
    n_queries = queries.shape[0]
    share = n_queries // n_mat

    def load(g):
        rows = pl.ds(g * group_rows, group_rows)
        return pltpu.make_async_copy(train_ref.at[rows], staged.at[g], load_sem.at[g])

    my_queries = pl.ds(pl.multiple_of(my_ex * 16, 16), 16)
    query_load = pltpu.make_async_copy(query_ref, queries.at[my_queries], query_load_sem)
    hess_load = pltpu.make_async_copy(hess_ref, hess, hess_sem)

    for g in range(GROUPS):
        load(g).start()
    query_load.start()
    hess_load.start()

    barrier = pltpu.get_barrier_semaphore()
    for k in range(1, n_mat):
        pl.semaphore_signal(
            barrier, inc=1, device_id={"mat": lax.rem(me + k, n_mat)}, device_id_type=MESH
        )
    for k in range(1, n_ex):
        pl.semaphore_signal(
            barrier, inc=1, device_id={"ex": lax.rem(my_ex + k, n_ex)}, device_id_type=MESH
        )

    out_row = lax.broadcasted_iota(jnp.int32, (group_rows, group_rows), 0)
    in_row = lax.broadcasted_iota(jnp.int32, (group_rows, group_rows), 1)
    regroup = jnp.where(
        in_row == lax.rem(out_row, part) * n_mat + out_row // part, 1.0, 0.0
    ).astype(BF16)
    mine = pl.ds(pl.multiple_of(me * part, part), part)

    def regroup_rows(g):
        load(g).wait()
        for c in range(columns // TILE):
            cols = pl.ds(c * TILE, TILE)
            outgoing[g, :, cols] = jnp.dot(
                regroup, staged[g, :, cols], preferred_element_type=F32
            ).astype(BF16)
        arrived[g, mine, :] = outgoing[g, mine, :]

    def send(g, i):
        to = peer(me, PEERS[i], 1)
        return pltpu.make_async_remote_copy(
            src_ref=outgoing.at[g, pl.ds(pl.multiple_of(to * part, part), part)],
            dst_ref=arrived.at[g, mine],
            send_sem=send_sem.at[g, i],
            recv_sem=recv_sem.at[g, i],
            device_id={"mat": to},
            device_id_type=MESH,
        )

    def arrival(g, i):
        source = peer(me, PEERS[i], -1)
        rows = pl.ds(pl.multiple_of(source * part, part), part)
        return pltpu.make_async_remote_copy(
            src_ref=outgoing.at[g, rows],
            dst_ref=arrived.at[g, rows],
            send_sem=send_sem.at[g, i],
            recv_sem=recv_sem.at[g, i],
            device_id={"mat": source},
            device_id_type=MESH,
        )

    def query_send(k):
        return pltpu.make_async_remote_copy(
            src_ref=queries.at[my_queries],
            dst_ref=queries.at[my_queries],
            send_sem=query_send_sem.at[k],
            recv_sem=query_recv_sem.at[k],
            device_id={"ex": lax.rem(my_ex + k, n_ex)},
            device_id_type=MESH,
        )

    def query_arrival(k):
        source = lax.rem(my_ex + n_ex - k, n_ex)
        rows = pl.ds(pl.multiple_of(source * 16, 16), 16)
        return pltpu.make_async_remote_copy(
            src_ref=queries.at[rows],
            dst_ref=queries.at[rows],
            send_sem=query_send_sem.at[k],
            recv_sem=query_recv_sem.at[k],
            device_id={"ex": source},
            device_id_type=MESH,
        )

    def x_copy(g):
        return pltpu.make_async_remote_copy(
            src_ref=x_out.at[g],
            dst_ref=x_in.at[g],
            send_sem=x_send_sem.at[g],
            recv_sem=x_recv_sem.at[g],
            device_id={"mat": peer(me, (1, 0), 1)},
            device_id_type=MESH,
        )

    def z_copy(g, k):
        to = peer(me, (0, k), 1)
        return pltpu.make_async_remote_copy(
            src_ref=z_out.at[g, pl.ds(pl.multiple_of(lax.rem(to, ZS) * share, share), share)],
            dst_ref=z_in.at[g, k],
            send_sem=z_send_sem.at[g, k],
            recv_sem=z_recv_sem.at[g, k],
            device_id={"mat": to},
            device_id_type=MESH,
        )

    def term_copy(i):
        to = peer(me, PEERS[i], 1)
        return pltpu.make_async_remote_copy(
            src_ref=last_out.at[pl.ds(pl.multiple_of(to * share, share), share)],
            dst_ref=last_in.at[i],
            send_sem=term_send_sem.at[i],
            recv_sem=term_recv_sem.at[i],
            device_id={"mat": to},
            device_id_type=MESH,
        )

    n_peers = len(PEERS)
    order = [(g, i) for g in range(GROUPS) for i in range(n_peers)]
    side, place = me // ZS, lax.rem(me, ZS)
    half = n_queries // 2
    my_half = pl.ds(pl.multiple_of(side * half, half), half)
    other_half = pl.ds(pl.multiple_of((1 - side) * half, half), half)
    my_share = pl.ds(pl.multiple_of(place * share, share), share)
    my_terms = pl.ds(pl.multiple_of(me * share, share), share)

    def multiply(g):
        def tile(c, carry):
            cols = pl.ds(pl.multiple_of(c * WIDE, WIDE), WIDE)
            product = jnp.dot(arrived[g], hess[:, cols], preferred_element_type=F32)
            pre_ref[:, pl.ds(g * part, part), cols] = product.astype(BF16).reshape(
                n_mat, part, WIDE
            )
            return carry

        lax.fori_loop(0, columns // WIDE, tile, 0)

    def scores_of(left, rows):
        return lax.dot_general(left, rows, (((1,), (1,)), ((), ())), preferred_element_type=F32)

    def start_terms(g):
        rows = pre_ref[:, pl.ds(g * part, part), :].reshape(group_rows, columns)
        terms[...] = scores_of(queries[...], rows)
        x_out[g] = terms[other_half, :].astype(BF16)
        x_copy(g).start()

    def pass_terms(g):
        x_copy(g).wait_recv()
        terms[my_half, :] = terms[my_half, :] + x_in[g].astype(F32)
        z_out[g] = terms[my_half, :].astype(BF16)
        for k in (4, 3, 5, 2, 6, 1, 7):
            z_copy(g, k).start()
        own[g] = terms[my_terms, :]

    lane = lax.broadcasted_iota(jnp.int32, (share, 128), 1)

    def place_scores(g, total):
        for j in range(scores_ref.shape[1] // 128):
            cols = pl.ds(j * 128, 128)
            tile = scores_ref[:, cols]
            for s in range(2):
                at, of = ((2 * j + s) * part) % 128, (2 * j + s) * part // 128
                to = s * (part * GROUPS) + g * part
                moved = pltpu.roll(total[:, of * 128 : of * 128 + 128], (to - at) % 128, 1)
                tile = jnp.where((lane >= to) & (lane < to + part), moved, tile)
            scores_ref[:, cols] = tile

    regroup_rows(0)
    query_load.wait()
    pl.semaphore_wait(barrier, n_mat + n_ex - 2)
    for j in range(AHEAD):
        send(*order[j]).start()
    for k in range(1, n_ex):
        query_send(k).start()
    for g in range(1, GROUPS):
        regroup_rows(g)
    scores_ref[...] = jnp.zeros_like(scores_ref)
    hess_load.wait()
    for k in range(1, n_ex):
        query_arrival(k).wait_recv()

    for j, (g, i) in enumerate(order):
        arrival(g, i).wait_recv()
        if j + AHEAD < len(order):
            send(*order[j + AHEAD]).start()
        if i == PASS_AT and g > 0:
            pass_terms(g - 1)
        if i == 3 and g == 1:

            def carry_back(c, carry):
                cols = pl.ds(pl.multiple_of(c * TILE, TILE), TILE)
                carried[:, cols] = scores_of(queries[...], hess[cols, :]).astype(BF16)
                return carry

            lax.fori_loop(0, columns // TILE, carry_back, 0)
        if i == n_peers - 1 and g < GROUPS - 1:
            multiply(g)
            start_terms(g)

    last = GROUPS - 1
    terms[...] = scores_of(carried[...], arrived[last])
    last_out[...] = terms[...].astype(BF16)
    for i in range(n_peers):
        term_copy(i).start()
    multiply(last)
    for g in range(last):
        total = own[g]
        for k in range(1, ZS):
            z_copy(g, k).wait_recv()
            total += z_in[g, k].astype(F32)
        place_scores(g, total)
    total = terms[my_terms, :]
    for i in range(n_peers):
        term_copy(i).wait_recv()
        total += last_in[i].astype(F32)
    place_scores(last, total)

    for g, i in order:
        send(g, i).wait_send()
    for k in range(1, n_ex):
        query_send(k).wait_send()
    for g in range(last):
        x_copy(g).wait_send()
        for k in range(1, ZS):
            z_copy(g, k).wait_send()
    for i in range(n_peers):
        term_copy(i).wait_send()


def in_hbm(array):
    return pltpu.with_memory_space_constraint(array, pltpu.HBM)


def on_device(n_ex, n_mat, train_grads, inverse_hessian, query_grads):
    rows, mats, columns = train_grads.shape
    all_rows = rows * mats
    group_rows = all_rows // GROUPS
    n_queries = query_grads.shape[0] * n_ex
    share = n_queries // n_mat
    dma = pltpu.SemaphoreType.DMA
    pre, scores = pl.pallas_call(
        functools.partial(kernel, n_ex, n_mat),
        name="influence",
        out_shape=(
            pltpu.VMEM((mats, rows, columns), BF16),
            jax.ShapeDtypeStruct((n_queries // n_mat, all_rows), F32),
        ),
        in_specs=[pl.BlockSpec(memory_space=pl.ANY)] * 3,
        out_specs=(
            pl.BlockSpec(memory_space=pltpu.VMEM),
            pl.BlockSpec(memory_space=pltpu.VMEM),
        ),
        scratch_shapes=[
            pltpu.VMEM((GROUPS, group_rows, columns), BF16),
            pltpu.VMEM((GROUPS, group_rows, columns), BF16),
            pltpu.VMEM((GROUPS, group_rows, columns), BF16),
            pltpu.VMEM((columns, columns), BF16),
            pltpu.VMEM((n_queries, columns), BF16),
            pltpu.VMEM((n_queries, columns), BF16),
            pltpu.VMEM((n_queries, group_rows), F32),
            pltpu.VMEM((GROUPS - 1, share, group_rows), F32),
            pltpu.VMEM((GROUPS - 1, n_queries // 2, group_rows), BF16),
            pltpu.VMEM((GROUPS - 1, n_queries // 2, group_rows), BF16),
            pltpu.VMEM((GROUPS - 1, n_queries // 2, group_rows), BF16),
            pltpu.VMEM((GROUPS - 1, ZS, share, group_rows), BF16),
            pltpu.VMEM((n_queries, group_rows), BF16),
            pltpu.VMEM((len(PEERS), share, group_rows), BF16),
            dma((GROUPS,)),
            dma,
            dma,
            dma((GROUPS, n_mat)),
            dma((GROUPS, n_mat)),
            dma((n_ex,)),
            dma((n_ex,)),
            dma((GROUPS - 1,)),
            dma((GROUPS - 1,)),
            dma((GROUPS - 1, ZS)),
            dma((GROUPS - 1, ZS)),
            dma((n_mat,)),
            dma((n_mat,)),
        ],
        compiler_params=pltpu.CompilerParams(
            collective_id=0, has_side_effects=True, vmem_limit_bytes=40 * 2**20
        ),
        cost_estimate=pl.CostEstimate(
            flops=2 * all_rows * columns * (columns + n_queries),
            bytes_accessed=2 * columns * (2 * all_rows + columns),
            transcendentals=0,
        ),
    )(
        in_hbm(train_grads.reshape(all_rows, columns)),
        in_hbm(inverse_hessian.reshape(columns, columns)),
        in_hbm(query_grads.reshape(query_grads.shape[0], columns)),
    )
    return pre.reshape(all_rows, 1, columns), scores


def solution(mesh):
    return jax.shard_map(
        functools.partial(on_device, mesh.shape["ex"], mesh.shape["mat"]),
        mesh=mesh,
        in_specs=(P(("ex", "mat"), None, None), P("mat", None, None), P("ex", "mat", None)),
        out_specs=(P("ex", "mat", None), P("mat", "ex")),
        check_vma=False,
    )
```

```python
import functools

import jax
import jax.numpy as jnp
from jax import lax
from jax.experimental import pallas as pl
from jax.experimental.pallas import tpu as pltpu
from jax.sharding import PartitionSpec as P

MESH = pl.DeviceIdType.MESH
F32, BF16 = jnp.float32, jnp.bfloat16
GROUPS = 4
ZS = 8
TILE = 512
WIDE = 1024
AHEAD = 22

PEERS = (
    (0, 4), (1, 4), (0, 3), (0, 5), (1, 3), (1, 5), (0, 2), (0, 6),
    (1, 2), (1, 6), (0, 1), (0, 7), (1, 1), (1, 7), (1, 0),
)


def peer(me, offset, sign):
    dx, dz = offset
    x, z = me // ZS, lax.rem(me, ZS)
    return lax.rem(x + dx, 2) * ZS + lax.rem(z + (dz if sign > 0 else ZS - dz), ZS)


def kernel(
    n_ex,
    n_mat,
    train_ref,
    hess_ref,
    query_ref,
    pre_ref,
    scores_ref,
    staged,
    outgoing,
    arrived,
    hess,
    queries,
    carried,
    terms,
    own,
    x_out,
    x_in,
    z_out,
    z_in,
    last_out,
    last_in,
    load_sem,
    hess_sem,
    query_load_sem,
    send_sem,
    recv_sem,
    query_send_sem,
    query_recv_sem,
    x_send_sem,
    x_recv_sem,
    z_send_sem,
    z_recv_sem,
    term_send_sem,
    term_recv_sem,
):
    me = lax.axis_index("mat")
    my_ex = lax.axis_index("ex")
    group_rows = train_ref.shape[0] // GROUPS
    part = group_rows // n_mat
    columns = train_ref.shape[1]
    n_queries = queries.shape[0]
    share = n_queries // n_mat

    def load(g):
        rows = pl.ds(g * group_rows, group_rows)
        return pltpu.make_async_copy(train_ref.at[rows], staged.at[g], load_sem.at[g])

    my_queries = pl.ds(pl.multiple_of(my_ex * 16, 16), 16)
    query_load = pltpu.make_async_copy(query_ref, queries.at[my_queries], query_load_sem)
    hess_load = pltpu.make_async_copy(hess_ref, hess, hess_sem)

    load(0).start()
    query_load.start()

    barrier = pltpu.get_barrier_semaphore()
    for k in range(1, n_mat):
        pl.semaphore_signal(
            barrier, inc=1, device_id={"mat": lax.rem(me + k, n_mat)}, device_id_type=MESH
        )
    for k in range(1, n_ex):
        pl.semaphore_signal(
            barrier, inc=1, device_id={"ex": lax.rem(my_ex + k, n_ex)}, device_id_type=MESH
        )

    out_row = lax.broadcasted_iota(jnp.int32, (group_rows, group_rows), 0)
    in_row = lax.broadcasted_iota(jnp.int32, (group_rows, group_rows), 1)
    regroup = jnp.where(
        in_row == lax.rem(out_row, part) * n_mat + out_row // part, 1.0, 0.0
    ).astype(BF16)
    mine = pl.ds(pl.multiple_of(me * part, part), part)

    def regroup_rows(g):
        load(g).wait()
        for c in range(columns // TILE):
            cols = pl.ds(c * TILE, TILE)
            outgoing[g, :, cols] = jnp.dot(
                regroup, staged[g, :, cols], preferred_element_type=F32
            ).astype(BF16)
        arrived[g, mine, :] = outgoing[g, mine, :]

    def send(g, i):
        to = peer(me, PEERS[i], 1)
        return pltpu.make_async_remote_copy(
            src_ref=outgoing.at[g, pl.ds(pl.multiple_of(to * part, part), part)],
            dst_ref=arrived.at[g, mine],
            send_sem=send_sem.at[g, i],
            recv_sem=recv_sem.at[g, i],
            device_id={"mat": to},
            device_id_type=MESH,
        )

    def arrival(g, i):
        source = peer(me, PEERS[i], -1)
        rows = pl.ds(pl.multiple_of(source * part, part), part)
        return pltpu.make_async_remote_copy(
            src_ref=outgoing.at[g, rows],
            dst_ref=arrived.at[g, rows],
            send_sem=send_sem.at[g, i],
            recv_sem=recv_sem.at[g, i],
            device_id={"mat": source},
            device_id_type=MESH,
        )

    def query_send(k):
        return pltpu.make_async_remote_copy(
            src_ref=queries.at[my_queries],
            dst_ref=queries.at[my_queries],
            send_sem=query_send_sem.at[k],
            recv_sem=query_recv_sem.at[k],
            device_id={"ex": lax.rem(my_ex + k, n_ex)},
            device_id_type=MESH,
        )

    def query_arrival(k):
        source = lax.rem(my_ex + n_ex - k, n_ex)
        rows = pl.ds(pl.multiple_of(source * 16, 16), 16)
        return pltpu.make_async_remote_copy(
            src_ref=queries.at[rows],
            dst_ref=queries.at[rows],
            send_sem=query_send_sem.at[k],
            recv_sem=query_recv_sem.at[k],
            device_id={"ex": source},
            device_id_type=MESH,
        )

    def x_copy(g):
        return pltpu.make_async_remote_copy(
            src_ref=x_out.at[g],
            dst_ref=x_in.at[g],
            send_sem=x_send_sem.at[g],
            recv_sem=x_recv_sem.at[g],
            device_id={"mat": peer(me, (1, 0), 1)},
            device_id_type=MESH,
        )

    def z_copy(g, k):
        to = peer(me, (0, k), 1)
        return pltpu.make_async_remote_copy(
            src_ref=z_out.at[g, pl.ds(pl.multiple_of(lax.rem(to, ZS) * share, share), share)],
            dst_ref=z_in.at[g, k],
            send_sem=z_send_sem.at[g, k],
            recv_sem=z_recv_sem.at[g, k],
            device_id={"mat": to},
            device_id_type=MESH,
        )

    def term_copy(i):
        to = peer(me, PEERS[i], 1)
        return pltpu.make_async_remote_copy(
            src_ref=last_out.at[pl.ds(pl.multiple_of(to * share, share), share)],
            dst_ref=last_in.at[i],
            send_sem=term_send_sem.at[i],
            recv_sem=term_recv_sem.at[i],
            device_id={"mat": to},
            device_id_type=MESH,
        )

    n_peers = len(PEERS)
    order = [(g, i) for g in range(GROUPS) for i in range(n_peers)]
    side, place = me // ZS, lax.rem(me, ZS)
    half = n_queries // 2
    my_half = pl.ds(pl.multiple_of(side * half, half), half)
    other_half = pl.ds(pl.multiple_of((1 - side) * half, half), half)
    my_share = pl.ds(pl.multiple_of(place * share, share), share)
    my_terms = pl.ds(pl.multiple_of(me * share, share), share)

    def multiply(g):
        def tile(c, carry):
            cols = pl.ds(pl.multiple_of(c * WIDE, WIDE), WIDE)
            product = jnp.dot(arrived[g], hess[:, cols], preferred_element_type=F32)
            pre_ref[:, pl.ds(g * part, part), cols] = product.astype(BF16).reshape(
                n_mat, part, WIDE
            )
            return carry

        lax.fori_loop(0, columns // WIDE, tile, 0)

    def scores_of(left, rows):
        return lax.dot_general(left, rows, (((1,), (1,)), ((), ())), preferred_element_type=F32)

    def start_terms(g):
        rows = pre_ref[:, pl.ds(g * part, part), :].reshape(group_rows, columns)
        terms[...] = scores_of(queries[...], rows)
        x_out[g] = terms[other_half, :].astype(BF16)
        x_copy(g).start()

    def pass_terms(g):
        x_copy(g).wait_recv()
        terms[my_half, :] = terms[my_half, :] + x_in[g].astype(F32)
        z_out[g] = terms[my_half, :].astype(BF16)
        for k in (4, 3, 5, 2, 6, 1, 7):
            z_copy(g, k).start()
        own[g] = terms[my_terms, :]

    lane = lax.broadcasted_iota(jnp.int32, (share, 128), 1)

    def place_scores(g, total):
        for j in range(scores_ref.shape[1] // 128):
            cols = pl.ds(j * 128, 128)
            tile = scores_ref[:, cols]
            for s in range(2):
                at, of = ((2 * j + s) * part) % 128, (2 * j + s) * part // 128
                to = s * (part * GROUPS) + g * part
                moved = pltpu.roll(total[:, of * 128 : of * 128 + 128], (to - at) % 128, 1)
                tile = jnp.where((lane >= to) & (lane < to + part), moved, tile)
            scores_ref[:, cols] = tile

    regroup_rows(0)
    query_load.wait()
    pl.semaphore_wait(barrier, n_mat + n_ex - 2)
    for i in range(n_peers):
        send(0, i).start()
        query_send(i + 1).start()
    for g in range(1, GROUPS):
        load(g).start()
    hess_load.start()
    regroup_rows(1)
    for j in range(n_peers, AHEAD):
        send(*order[j]).start()
    for g in range(2, GROUPS):
        regroup_rows(g)
    scores_ref[...] = jnp.zeros_like(scores_ref)
    hess_load.wait()
    for k in range(1, n_ex):
        query_arrival(k).wait_recv()

    for j, (g, i) in enumerate(order):
        arrival(g, i).wait_recv()
        if j + AHEAD < len(order):
            send(*order[j + AHEAD]).start()
        if i == 3 and g == 1:

            def carry_back(c, carry):
                cols = pl.ds(pl.multiple_of(c * TILE, TILE), TILE)
                carried[:, cols] = scores_of(queries[...], hess[cols, :]).astype(BF16)
                return carry

            lax.fori_loop(0, columns // TILE, carry_back, 0)
        if i == n_peers - 1 and g < GROUPS - 1:
            multiply(g)
            if g > 0:
                pass_terms(g - 1)
            start_terms(g)

    last = GROUPS - 1
    pass_terms(last - 1)
    terms[...] = scores_of(carried[...], arrived[last])
    last_out[...] = terms[...].astype(BF16)
    for i in range(n_peers):
        term_copy(i).start()
    multiply(last)
    for g in range(last):
        total = own[g]
        for k in range(1, ZS):
            z_copy(g, k).wait_recv()
            total += z_in[g, k].astype(F32)
        place_scores(g, total)
    total = terms[my_terms, :]
    for i in range(n_peers):
        term_copy(i).wait_recv()
        total += last_in[i].astype(F32)
    place_scores(last, total)

    for g, i in order:
        send(g, i).wait_send()
    for i in range(n_peers):
        query_send(i + 1).wait_send()
    for g in range(last):
        x_copy(g).wait_send()
        for k in range(1, ZS):
            z_copy(g, k).wait_send()
    for i in range(n_peers):
        term_copy(i).wait_send()


def in_hbm(array):
    return pltpu.with_memory_space_constraint(array, pltpu.HBM)


def on_device(n_ex, n_mat, train_grads, inverse_hessian, query_grads):
    rows, mats, columns = train_grads.shape
    all_rows = rows * mats
    group_rows = all_rows // GROUPS
    n_queries = query_grads.shape[0] * n_ex
    share = n_queries // n_mat
    dma = pltpu.SemaphoreType.DMA
    pre, scores = pl.pallas_call(
        functools.partial(kernel, n_ex, n_mat),
        name="influence",
        out_shape=(
            pltpu.VMEM((mats, rows, columns), BF16),
            jax.ShapeDtypeStruct((n_queries // n_mat, all_rows), F32),
        ),
        in_specs=[pl.BlockSpec(memory_space=pl.ANY)] * 3,
        out_specs=(
            pl.BlockSpec(memory_space=pltpu.VMEM),
            pl.BlockSpec(memory_space=pltpu.VMEM),
        ),
        scratch_shapes=[
            pltpu.VMEM((GROUPS, group_rows, columns), BF16),
            pltpu.VMEM((GROUPS, group_rows, columns), BF16),
            pltpu.VMEM((GROUPS, group_rows, columns), BF16),
            pltpu.VMEM((columns, columns), BF16),
            pltpu.VMEM((n_queries, columns), BF16),
            pltpu.VMEM((n_queries, columns), BF16),
            pltpu.VMEM((n_queries, group_rows), F32),
            pltpu.VMEM((GROUPS - 1, share, group_rows), F32),
            pltpu.VMEM((GROUPS - 1, n_queries // 2, group_rows), BF16),
            pltpu.VMEM((GROUPS - 1, n_queries // 2, group_rows), BF16),
            pltpu.VMEM((GROUPS - 1, n_queries // 2, group_rows), BF16),
            pltpu.VMEM((GROUPS - 1, ZS, share, group_rows), BF16),
            pltpu.VMEM((n_queries, group_rows), BF16),
            pltpu.VMEM((len(PEERS), share, group_rows), BF16),
            dma((GROUPS,)),
            dma,
            dma,
            dma((GROUPS, n_mat)),
            dma((GROUPS, n_mat)),
            dma((n_ex,)),
            dma((n_ex,)),
            dma((GROUPS - 1,)),
            dma((GROUPS - 1,)),
            dma((GROUPS - 1, ZS)),
            dma((GROUPS - 1, ZS)),
            dma((n_mat,)),
            dma((n_mat,)),
        ],
        compiler_params=pltpu.CompilerParams(
            collective_id=0, has_side_effects=True, vmem_limit_bytes=40 * 2**20
        ),
        cost_estimate=pl.CostEstimate(
            flops=2 * all_rows * columns * (columns + n_queries),
            bytes_accessed=2 * columns * (2 * all_rows + columns),
            transcendentals=0,
        ),
    )(
        in_hbm(train_grads.reshape(all_rows, columns)),
        in_hbm(inverse_hessian.reshape(columns, columns)),
        in_hbm(query_grads.reshape(query_grads.shape[0], columns)),
    )
    return pre.reshape(all_rows, 1, columns), scores


def solution(mesh):
    return jax.shard_map(
        functools.partial(on_device, mesh.shape["ex"], mesh.shape["mat"]),
        mesh=mesh,
        in_specs=(P(("ex", "mat"), None, None), P("mat", None, None), P("ex", "mat", None)),
        out_specs=(P("ex", "mat", None), P("mat", "ex")),
        check_vma=False,
    )
```

```python
import functools

import jax
import jax.numpy as jnp
from jax import lax
from jax.experimental import pallas as pl
from jax.experimental.pallas import tpu as pltpu
from jax.sharding import PartitionSpec as P

MESH = pl.DeviceIdType.MESH
F32, BF16 = jnp.float32, jnp.bfloat16
GROUPS = 4
LAST = GROUPS - 1
ZS = 8
TILE = 512
WIDE = 1024

PEERS = (
    (0, 4), (1, 4), (0, 3), (0, 5), (1, 3), (1, 5), (0, 2), (0, 6),
    (1, 2), (1, 6), (0, 1), (0, 7), (1, 1), (1, 7), (1, 0),
)
Z_PEERS = (4, 3, 5, 2, 6, 1, 7)


def kernel(
    n_ex,
    n_mat,
    train_ref,
    hess_ref,
    query_ref,
    pre_ref,
    own,
    z_in,
    last_in,
    staged,
    outgoing,
    arrived,
    hess,
    queries,
    carried,
    terms,
    x_out,
    x_in,
    z_out,
    last_out,
    load_sem,
    hess_sem,
    query_load_sem,
    send_sem,
    recv_sem,
    query_send_sem,
    query_recv_sem,
    x_send_sem,
    x_recv_sem,
    z_send_sem,
    z_recv_sem,
    term_send_sem,
    term_recv_sem,
):
    me = lax.axis_index("mat")
    my_ex = lax.axis_index("ex")
    side, place = me // ZS, lax.rem(me, ZS)
    z_at = [place] + [lax.rem(place + k, ZS) for k in range(1, ZS)]
    x_at = [side, 1 - side]
    peers = [x_at[dx] * ZS + z_at[dz] for dx, dz in PEERS]
    n_peers = len(PEERS)

    group_rows = train_ref.shape[0] // GROUPS
    part = group_rows // n_mat
    columns = train_ref.shape[1]
    n_queries = queries.shape[0]
    share = n_queries // n_mat
    half = n_queries // 2
    ex_share = query_ref.shape[0]

    mine = pl.ds(pl.multiple_of(me * part, part), part)
    my_queries = pl.ds(pl.multiple_of(my_ex * ex_share, ex_share), ex_share)
    my_half = pl.ds(pl.multiple_of(side * half, half), half)
    other_half = pl.ds(pl.multiple_of((1 - side) * half, half), half)
    my_terms = pl.ds(pl.multiple_of(me * share, share), share)

    def load(g):
        rows = pl.ds(g * group_rows, group_rows)
        return pltpu.make_async_copy(train_ref.at[rows], staged.at[g], load_sem.at[g])

    query_load = pltpu.make_async_copy(query_ref, queries.at[my_queries], query_load_sem)
    hess_load = pltpu.make_async_copy(hess_ref, hess, hess_sem)

    load(0).start()
    query_load.start()
    barrier = pltpu.get_barrier_semaphore()
    for to in peers:
        pl.semaphore_signal(barrier, inc=1, device_id={"mat": to}, device_id_type=MESH)
    ex_peers = [lax.rem(my_ex + k, n_ex) for k in range(1, n_ex)]
    for to in ex_peers:
        pl.semaphore_signal(barrier, inc=1, device_id={"ex": to}, device_id_type=MESH)

    out_row = lax.broadcasted_iota(jnp.int32, (group_rows, group_rows), 0)
    in_row = lax.broadcasted_iota(jnp.int32, (group_rows, group_rows), 1)
    regroup = jnp.where(
        in_row == lax.rem(out_row, part) * n_mat + out_row // part, 1.0, 0.0
    ).astype(BF16)

    def regroup_rows(g):
        load(g).wait()
        for c in range(columns // TILE):
            cols = pl.ds(c * TILE, TILE)
            outgoing[g, :, cols] = jnp.dot(
                regroup, staged[g, :, cols], preferred_element_type=F32
            ).astype(BF16)
        arrived[g, mine, :] = outgoing[g, mine, :]

    def to_mat(src, dst, sent, received, device):
        return pltpu.make_async_remote_copy(
            src_ref=src,
            dst_ref=dst,
            send_sem=sent,
            recv_sem=received,
            device_id={"mat": device},
            device_id_type=MESH,
        )

    def send(g, i):
        rows = pl.ds(pl.multiple_of(peers[i] * part, part), part)
        return to_mat(
            outgoing.at[g, rows], arrived.at[g, mine], send_sem.at[g], recv_sem.at[g], peers[i]
        )

    def all_sends(g):
        rows = pl.ds(0, part * n_peers)
        return to_mat(
            outgoing.at[g, rows], arrived.at[g, rows], send_sem.at[g], recv_sem.at[g], peers[0]
        )

    def to_ex(rows, device):
        return pltpu.make_async_remote_copy(
            src_ref=queries.at[rows],
            dst_ref=queries.at[rows],
            send_sem=query_send_sem,
            recv_sem=query_recv_sem,
            device_id={"ex": device},
            device_id_type=MESH,
        )

    all_query_sends = to_ex(pl.ds(0, ex_share * (n_ex - 1)), ex_peers[0])

    def x_copy(g):
        return to_mat(x_out.at[g], x_in.at[g], x_send_sem.at[g], x_recv_sem.at[g], peers[-1])

    def z_copy(g, i):
        to = z_at[Z_PEERS[i]]
        return to_mat(
            z_out.at[g, pl.ds(pl.multiple_of(to * share, share), share)],
            z_in.at[g, i],
            z_send_sem.at[g],
            z_recv_sem.at[g],
            side * ZS + to,
        )

    def all_z(g):
        slots = pl.ds(0, len(Z_PEERS))
        return to_mat(
            z_in.at[g, slots], z_in.at[g, slots], z_send_sem.at[g], z_recv_sem.at[g], peers[0]
        )

    def term_copy(i):
        rows = pl.ds(pl.multiple_of(peers[i] * share, share), share)
        return to_mat(last_out.at[rows], last_in.at[i], term_send_sem, term_recv_sem, peers[i])

    all_terms = to_mat(last_in, last_in, term_send_sem, term_recv_sem, peers[0])

    def multiply(g):
        def tile(c, carry):
            cols = pl.ds(pl.multiple_of(c * WIDE, WIDE), WIDE)
            product = jnp.dot(arrived[g], hess[:, cols], preferred_element_type=F32)
            pre_ref[:, pl.ds(g * part, part), cols] = product.astype(BF16).reshape(
                n_mat, part, WIDE
            )
            return carry

        lax.fori_loop(0, columns // WIDE, tile, 0)

    def scores_of(left, rows):
        return lax.dot_general(left, rows, (((1,), (1,)), ((), ())), preferred_element_type=F32)

    def start_terms(g):
        rows = pre_ref[:, pl.ds(g * part, part), :].reshape(group_rows, columns)
        terms[...] = scores_of(queries[...], rows)
        x_out[g] = terms[other_half, :].astype(BF16)
        x_copy(g).start()

    def pass_terms(g):
        x_copy(g).wait_recv()
        terms[my_half, :] = terms[my_half, :] + x_in[g].astype(F32)
        z_out[g] = terms[my_half, :].astype(BF16)
        for i in range(len(Z_PEERS)):
            z_copy(g, i).start()
        own[g] = terms[my_terms, :]

    regroup_rows(0)
    query_load.wait()
    pl.semaphore_wait(barrier, n_mat + n_ex - 2)
    for i in range(n_peers):
        send(0, i).start()
        to_ex(my_queries, ex_peers[i]).start()
    for g in range(1, GROUPS):
        load(g).start()
    hess_load.start()
    regroup_rows(1)
    for i in range(n_peers):
        send(1, i).start()
    for g in range(2, GROUPS):
        regroup_rows(g)
    hess_load.wait()
    all_query_sends.wait_recv()

    for g in range(GROUPS):
        all_sends(g).wait_recv()
        if g + 2 < GROUPS:
            for i in range(n_peers):
                send(g + 2, i).start()
        if g < LAST:
            multiply(g)
            if g > 0:
                pass_terms(g - 1)
            start_terms(g)
        if g == 0:
            all_query_sends.wait_send()

            def carry_back(c, carry):
                cols = pl.ds(pl.multiple_of(c * TILE, TILE), TILE)
                carried[:, cols] = scores_of(queries[...], hess[cols, :]).astype(BF16)
                return carry

            lax.fori_loop(0, columns // TILE, carry_back, 0)
        else:
            all_sends(g - 1).wait_send()

    pass_terms(LAST - 1)
    terms[...] = scores_of(carried[...], arrived[LAST])
    last_out[...] = terms[...].astype(BF16)
    for i in range(n_peers):
        term_copy(i).start()
    own[LAST] = terms[my_terms, :]
    multiply(LAST)

    all_sends(LAST).wait_send()
    for g in range(LAST):
        x_copy(g).wait_send()
        all_z(g).wait_send()
        all_z(g).wait_recv()
    all_terms.wait_send()
    all_terms.wait_recv()


def finish(pre_ref, own, z_in, last_in, out_ref, scores_ref, scores, out_sem, scores_sem):
    n_mat = pre_ref.shape[0]
    pieces = out_sem.shape[0]
    step = n_mat // pieces
    part = own.shape[2] // n_mat

    def out_copy(k):
        mats = pl.ds(k * step, step)
        return pltpu.make_async_copy(pre_ref.at[mats], out_ref.at[mats], out_sem.at[k])

    for k in range(pieces):
        out_copy(k).start()
    totals = []
    for g in range(GROUPS):
        total = own[g]
        if g < LAST:
            for i in range(len(Z_PEERS)):
                total += z_in[g, i].astype(F32)
        else:
            for i in range(len(PEERS)):
                total += last_in[i].astype(F32)
        totals.append(total)
    lane = lax.broadcasted_iota(jnp.int32, (own.shape[1], 128), 1)
    for j in range(scores.shape[1] // 128):
        tile = jnp.zeros(lane.shape, F32)
        for s in range(2):
            at, of = ((2 * j + s) * part) % 128, (2 * j + s) * part // 128
            for g in range(GROUPS):
                to = (s * GROUPS + g) * part
                moved = pltpu.roll(totals[g][:, of * 128 : of * 128 + 128], (to - at) % 128, 1)
                tile = jnp.where((lane >= to) & (lane < to + part), moved, tile)
        scores[:, j * 128 : j * 128 + 128] = tile
    scores_copy = pltpu.make_async_copy(scores, scores_ref, scores_sem)
    scores_copy.start()
    for k in range(pieces):
        out_copy(k).wait()
    scores_copy.wait()


def in_hbm(array):
    return pltpu.with_memory_space_constraint(array, pltpu.HBM)


def on_device(n_ex, n_mat, train_grads, inverse_hessian, query_grads):
    rows, mats, columns = train_grads.shape
    all_rows = rows * mats
    group_rows = all_rows // GROUPS
    n_queries = query_grads.shape[0] * n_ex
    share = n_queries // n_mat
    dma = pltpu.SemaphoreType.DMA
    in_vmem = pl.BlockSpec(memory_space=pltpu.VMEM)
    anywhere = pl.BlockSpec(memory_space=pl.ANY)
    parts = pl.pallas_call(
        functools.partial(kernel, n_ex, n_mat),
        name="influence",
        out_shape=(
            pltpu.VMEM((mats, rows, columns), BF16),
            pltpu.VMEM((GROUPS, share, group_rows), F32),
            pltpu.VMEM((LAST, len(Z_PEERS), share, group_rows), BF16),
            pltpu.VMEM((len(PEERS), share, group_rows), BF16),
        ),
        in_specs=[anywhere] * 3,
        out_specs=(in_vmem,) * 4,
        scratch_shapes=[
            pltpu.VMEM((GROUPS, group_rows, columns), BF16),
            pltpu.VMEM((GROUPS, group_rows, columns), BF16),
            pltpu.VMEM((GROUPS, group_rows, columns), BF16),
            pltpu.VMEM((columns, columns), BF16),
            pltpu.VMEM((n_queries, columns), BF16),
            pltpu.VMEM((n_queries, columns), BF16),
            pltpu.VMEM((n_queries, group_rows), F32),
            pltpu.VMEM((LAST, n_queries // 2, group_rows), BF16),
            pltpu.VMEM((LAST, n_queries // 2, group_rows), BF16),
            pltpu.VMEM((LAST, n_queries // 2, group_rows), BF16),
            pltpu.VMEM((n_queries, group_rows), BF16),
            dma((GROUPS,)),
            dma,
            dma,
            dma((GROUPS,)),
            dma((GROUPS,)),
            dma,
            dma,
            dma((LAST,)),
            dma((LAST,)),
            dma((LAST,)),
            dma((LAST,)),
            dma,
            dma,
        ],
        compiler_params=pltpu.CompilerParams(
            collective_id=0, has_side_effects=True, vmem_limit_bytes=40 * 2**20
        ),
        cost_estimate=pl.CostEstimate(
            flops=2 * all_rows * columns * (columns + n_queries),
            bytes_accessed=2 * columns * (2 * all_rows + columns),
            transcendentals=0,
        ),
    )(
        in_hbm(train_grads.reshape(all_rows, columns)),
        in_hbm(inverse_hessian.reshape(columns, columns)),
        in_hbm(query_grads.reshape(query_grads.shape[0], columns)),
    )
    pre, scores = pl.pallas_call(
        finish,
        name="write_out",
        out_shape=(
            pltpu.HBM((mats, rows, columns), BF16),
            pltpu.HBM((share, all_rows), F32),
        ),
        in_specs=[in_vmem] * 4,
        out_specs=(anywhere,) * 2,
        scratch_shapes=[pltpu.VMEM((share, all_rows), F32), dma((4,)), dma],
        compiler_params=pltpu.CompilerParams(vmem_limit_bytes=16 * 2**20),
    )(*parts)
    return pre.reshape(all_rows, 1, columns), scores


def solution(mesh):
    return jax.shard_map(
        functools.partial(on_device, mesh.shape["ex"], mesh.shape["mat"]),
        mesh=mesh,
        in_specs=(P(("ex", "mat"), None, None), P("mat", None, None), P("ex", "mat", None)),
        out_specs=(P("ex", "mat", None), P("mat", "ex")),
        check_vma=False,
    )
```

```python
import functools

import jax
import jax.numpy as jnp
from jax import lax
from jax.experimental import pallas as pl
from jax.experimental.pallas import tpu as pltpu
from jax.sharding import PartitionSpec as P

MESH = pl.DeviceIdType.MESH
F32, BF16 = jnp.float32, jnp.bfloat16
GROUPS = 4
LAST = GROUPS - 1
ZS = 8
TILE = 512
WIDE = 1024

PEERS = (
    (0, 4), (1, 4), (0, 3), (0, 5), (1, 3), (1, 5), (0, 2), (0, 6),
    (1, 2), (1, 6), (0, 1), (0, 7), (1, 1), (1, 7), (1, 0),
)
Z_PEERS = (4, 3, 5, 2, 6, 1, 7)
SAME = tuple(i for i, (dx, dz) in enumerate(PEERS) if dz % 2 == 0)
OTHER = tuple(i for i, (dx, dz) in enumerate(PEERS) if dz % 2 == 1)


def kernel(
    n_ex,
    n_mat,
    train_ref,
    hess_ref,
    query_ref,
    pre_ref,
    own,
    own_last,
    z_in,
    last_in,
    staged,
    outgoing,
    arrived,
    hess,
    queries,
    carried,
    terms,
    x_out,
    x_in,
    z_out,
    last_out,
    last_terms_out,
    load_sem,
    hess_sem,
    query_load_sem,
    send_sem,
    recv_sem,
    query_send_sem,
    query_recv_sem,
    x_send_sem,
    x_recv_sem,
    z_send_sem,
    z_recv_sem,
    term_send_sem,
    term_recv_sem,
):
    me = lax.axis_index("mat")
    my_ex = lax.axis_index("ex")
    side, place = me // ZS, lax.rem(me, ZS)
    z_at = [place] + [lax.rem(place + k, ZS) for k in range(1, ZS)]
    x_at = [side, 1 - side]
    peers = [x_at[dx] * ZS + z_at[dz] for dx, dz in PEERS]
    n_peers = len(PEERS)

    group_rows = train_ref.shape[0] // GROUPS
    part = group_rows // n_mat
    columns = train_ref.shape[1]
    n_queries = queries.shape[0]
    share = n_queries // n_mat
    half = n_queries // 2
    ex_share = query_ref.shape[0]

    parity = lax.rem(place, 2)
    mine = pl.ds(pl.multiple_of(me * part, part), part)
    slot = parity * (n_mat // 2) + side * (ZS // 2) + place // 2
    my_slot = pl.ds(pl.multiple_of(slot * part, part), part)
    my_queries = pl.ds(pl.multiple_of(my_ex * ex_share, ex_share), ex_share)
    my_half = pl.ds(pl.multiple_of(side * half, half), half)
    other_half = pl.ds(pl.multiple_of((1 - side) * half, half), half)
    my_terms = pl.ds(pl.multiple_of(me * share, share), share)

    def load(g):
        rows = pl.ds(g * group_rows, group_rows)
        return pltpu.make_async_copy(train_ref.at[rows], staged.at[g], load_sem.at[g])

    query_load = pltpu.make_async_copy(query_ref, queries.at[my_queries], query_load_sem)
    hess_load = pltpu.make_async_copy(hess_ref, hess, hess_sem)

    load(0).start()
    query_load.start()
    barrier = pltpu.get_barrier_semaphore()
    for to in peers:
        pl.semaphore_signal(barrier, inc=1, device_id={"mat": to}, device_id_type=MESH)
    ex_peers = [lax.rem(my_ex + k, n_ex) for k in range(1, n_ex)]
    for to in ex_peers:
        pl.semaphore_signal(barrier, inc=1, device_id={"ex": to}, device_id_type=MESH)

    out_row = lax.broadcasted_iota(jnp.int32, (group_rows, group_rows), 0)
    in_row = lax.broadcasted_iota(jnp.int32, (group_rows, group_rows), 1)
    regroup = jnp.where(
        in_row == lax.rem(out_row, part) * n_mat + out_row // part, 1.0, 0.0
    ).astype(BF16)

    def regroup_rows(g):
        load(g).wait()
        for c in range(columns // TILE):
            cols = pl.ds(c * TILE, TILE)
            outgoing[g, :, cols] = jnp.dot(
                regroup, staged[g, :, cols], preferred_element_type=F32
            ).astype(BF16)
        arrived[g, my_slot, :] = outgoing[g, mine, :]

    def to_mat(src, dst, sent, received, device):
        return pltpu.make_async_remote_copy(
            src_ref=src,
            dst_ref=dst,
            send_sem=sent,
            recv_sem=received,
            device_id={"mat": device},
            device_id_type=MESH,
        )

    def send(g, i):
        rows = pl.ds(pl.multiple_of(peers[i] * part, part), part)
        k = g + 1 if g == LAST and i in OTHER else g
        return to_mat(
            outgoing.at[g, rows], arrived.at[g, my_slot], send_sem.at[k], recv_sem.at[k], peers[i]
        )

    def all_sends(k):
        count = n_peers if k < LAST else len(SAME) if k == LAST else len(OTHER)
        rows = pl.ds(0, part * count)
        g = min(k, LAST)
        return to_mat(
            outgoing.at[g, rows], arrived.at[g, rows], send_sem.at[k], recv_sem.at[k], peers[0]
        )

    def to_ex(rows, device):
        return pltpu.make_async_remote_copy(
            src_ref=queries.at[rows],
            dst_ref=queries.at[rows],
            send_sem=query_send_sem,
            recv_sem=query_recv_sem,
            device_id={"ex": device},
            device_id_type=MESH,
        )

    all_query_sends = to_ex(pl.ds(0, ex_share * (n_ex - 1)), ex_peers[0])

    def x_copy(g):
        return to_mat(x_out.at[g], x_in.at[g], x_send_sem.at[g], x_recv_sem.at[g], peers[-1])

    def z_copy(g, i):
        to = z_at[Z_PEERS[i]]
        return to_mat(
            z_out.at[g, pl.ds(pl.multiple_of(to * share, share), share)],
            z_in.at[g, i],
            z_send_sem.at[g],
            z_recv_sem.at[g],
            side * ZS + to,
        )

    def all_z(g):
        slots = pl.ds(0, len(Z_PEERS))
        return to_mat(
            z_in.at[g, slots], z_in.at[g, slots], z_send_sem.at[g], z_recv_sem.at[g], peers[0]
        )

    def term_copy(h, i):
        rows = pl.ds(pl.multiple_of(peers[i] * share, share), share)
        to = parity if h == 0 else 1 - parity
        return to_mat(
            last_out.at[h, rows], last_in.at[i, to], term_send_sem, term_recv_sem, peers[i]
        )

    all_terms = to_mat(last_in, last_in, term_send_sem, term_recv_sem, peers[0])

    def multiply(g):
        def tile(c, carry):
            cols = pl.ds(pl.multiple_of(c * WIDE, WIDE), WIDE)
            product = jnp.dot(arrived[g], hess[:, cols], preferred_element_type=F32)
            product = product.astype(BF16).reshape(n_mat, part, WIDE)
            for at in range(n_mat):
                odd, x, z = at // (n_mat // 2), at // (ZS // 2) % 2, at % (ZS // 2)
                pre_ref[x * ZS + 2 * z + odd, pl.ds(g * part, part), cols] = product[at]
            return carry

        lax.fori_loop(0, columns // WIDE, tile, 0)

    def scores_of(left, rows):
        return lax.dot_general(left, rows, (((1,), (1,)), ((), ())), preferred_element_type=F32)

    def start_terms(g):
        rows = pre_ref[:, pl.ds(g * part, part), :].reshape(group_rows, columns)
        terms[...] = scores_of(queries[...], rows)
        x_out[g] = terms[other_half, :].astype(BF16)
        x_copy(g).start()

    def pass_terms(g):
        x_copy(g).wait_recv()
        terms[my_half, :] = terms[my_half, :] + x_in[g].astype(F32)
        z_out[g] = terms[my_half, :].astype(BF16)
        for i in range(len(Z_PEERS)):
            z_copy(g, i).start()
        own[g] = terms[my_terms, :]

    regroup_rows(0)
    query_load.wait()
    pl.semaphore_wait(barrier, n_mat + n_ex - 2)
    for i in range(n_peers):
        send(0, i).start()
        to_ex(my_queries, ex_peers[i]).start()
    for g in range(1, GROUPS):
        load(g).start()
    hess_load.start()
    regroup_rows(1)
    for i in range(n_peers):
        send(1, i).start()
    for g in range(2, GROUPS):
        regroup_rows(g)
    hess_load.wait()
    all_query_sends.wait_recv()

    def last_terms(h):
        at = parity if h == 0 else 1 - parity
        rows = pl.ds(pl.multiple_of(at * (group_rows // 2), group_rows // 2), group_rows // 2)
        product = scores_of(carried[...], arrived[LAST, rows, :])
        last_terms_out[...] = product
        last_out[h] = product.astype(BF16)
        for i in range(n_peers):
            term_copy(h, i).start()
        own_last[at] = last_terms_out[my_terms, :]

    for g in range(LAST):
        all_sends(g).wait_recv()
        multiply(g)
        if g > 0:
            pass_terms(g - 1)
        start_terms(g)
        for i in range(n_peers) if g == 0 else SAME if g == 1 else OTHER:
            send(min(g + 2, LAST), i).start()
        if g == 0:
            all_query_sends.wait_send()

            def carry_back(c, carry):
                cols = pl.ds(pl.multiple_of(c * TILE, TILE), TILE)
                carried[:, cols] = scores_of(queries[...], hess[cols, :]).astype(BF16)
                return carry

            lax.fori_loop(0, columns // TILE, carry_back, 0)
        else:
            all_sends(g - 1).wait_send()

    all_sends(LAST).wait_recv()
    last_terms(0)
    pass_terms(LAST - 1)
    all_sends(LAST + 1).wait_recv()
    last_terms(1)
    multiply(LAST)

    for k in range(LAST - 1, LAST + 2):
        all_sends(k).wait_send()
    for g in range(LAST):
        x_copy(g).wait_send()
        all_z(g).wait_send()
        all_z(g).wait_recv()
    all_terms.wait_send()
    all_terms.wait_recv()


def finish(pre_ref, own, own_last, z_in, last_in, out_ref, scores_ref, scores, out_sem, scores_sem):
    n_mat = pre_ref.shape[0]
    pieces = out_sem.shape[0]
    step = n_mat // pieces
    part = own.shape[2] // n_mat

    def out_copy(k):
        mats = pl.ds(k * step, step)
        return pltpu.make_async_copy(pre_ref.at[mats], out_ref.at[mats], out_sem.at[k])

    for k in range(pieces):
        out_copy(k).start()
    totals = []
    for g in range(LAST):
        total = own[g]
        for i in range(len(Z_PEERS)):
            total += z_in[g, i].astype(F32)
        totals += [total[:, :128], total[:, 128:]]
    for h in range(2):
        total = own_last[h]
        for i in range(len(PEERS)):
            total += last_in[i, h].astype(F32)
        totals.append(total)
    lane = lax.broadcasted_iota(jnp.int32, (own.shape[1], 128), 1)
    for j in range(n_mat // 2):
        tile = jnp.zeros(lane.shape, F32)
        for s in range(2):
            mat = 2 * j + s
            for g in range(GROUPS):
                x, z = mat // ZS, mat % ZS
                slot = mat if g < LAST else z % 2 * (n_mat // 2) + x * (ZS // 2) + z // 2
                at, half = (slot * part) % 128, slot * part // 128
                to = (s * GROUPS + g) * part
                moved = pltpu.roll(totals[2 * g + half], (to - at) % 128, 1)
                tile = jnp.where((lane >= to) & (lane < to + part), moved, tile)
        scores[:, j * 128 : j * 128 + 128] = tile
    scores_copy = pltpu.make_async_copy(scores, scores_ref, scores_sem)
    scores_copy.start()
    for k in range(pieces):
        out_copy(k).wait()
    scores_copy.wait()


def in_hbm(array):
    return pltpu.with_memory_space_constraint(array, pltpu.HBM)


def on_device(n_ex, n_mat, train_grads, inverse_hessian, query_grads):
    rows, mats, columns = train_grads.shape
    all_rows = rows * mats
    group_rows = all_rows // GROUPS
    n_queries = query_grads.shape[0] * n_ex
    share = n_queries // n_mat
    dma = pltpu.SemaphoreType.DMA
    in_vmem = pl.BlockSpec(memory_space=pltpu.VMEM)
    anywhere = pl.BlockSpec(memory_space=pl.ANY)
    parts = pl.pallas_call(
        functools.partial(kernel, n_ex, n_mat),
        name="influence",
        out_shape=(
            pltpu.VMEM((mats, rows, columns), BF16),
            pltpu.VMEM((LAST, share, group_rows), F32),
            pltpu.VMEM((2, share, group_rows // 2), F32),
            pltpu.VMEM((LAST, len(Z_PEERS), share, group_rows), BF16),
            pltpu.VMEM((len(PEERS), 2, share, group_rows // 2), BF16),
        ),
        in_specs=[anywhere] * 3,
        out_specs=(in_vmem,) * 5,
        scratch_shapes=[
            pltpu.VMEM((GROUPS, group_rows, columns), BF16),
            pltpu.VMEM((GROUPS, group_rows, columns), BF16),
            pltpu.VMEM((GROUPS, group_rows, columns), BF16),
            pltpu.VMEM((columns, columns), BF16),
            pltpu.VMEM((n_queries, columns), BF16),
            pltpu.VMEM((n_queries, columns), BF16),
            pltpu.VMEM((n_queries, group_rows), F32),
            pltpu.VMEM((LAST, n_queries // 2, group_rows), BF16),
            pltpu.VMEM((LAST, n_queries // 2, group_rows), BF16),
            pltpu.VMEM((LAST, n_queries // 2, group_rows), BF16),
            pltpu.VMEM((2, n_queries, group_rows // 2), BF16),
            pltpu.VMEM((n_queries, group_rows // 2), F32),
            dma((GROUPS,)),
            dma,
            dma,
            dma((GROUPS + 1,)),
            dma((GROUPS + 1,)),
            dma,
            dma,
            dma((LAST,)),
            dma((LAST,)),
            dma((LAST,)),
            dma((LAST,)),
            dma,
            dma,
        ],
        compiler_params=pltpu.CompilerParams(
            collective_id=0, has_side_effects=True, vmem_limit_bytes=40 * 2**20
        ),
        cost_estimate=pl.CostEstimate(
            flops=2 * all_rows * columns * (columns + n_queries),
            bytes_accessed=2 * columns * (2 * all_rows + columns),
            transcendentals=0,
        ),
    )(
        in_hbm(train_grads.reshape(all_rows, columns)),
        in_hbm(inverse_hessian.reshape(columns, columns)),
        in_hbm(query_grads.reshape(query_grads.shape[0], columns)),
    )
    pre, scores = pl.pallas_call(
        finish,
        name="write_out",
        out_shape=(
            pltpu.HBM((mats, rows, columns), BF16),
            pltpu.HBM((share, all_rows), F32),
        ),
        in_specs=[in_vmem] * 5,
        out_specs=(anywhere,) * 2,
        scratch_shapes=[pltpu.VMEM((share, all_rows), F32), dma((4,)), dma],
        compiler_params=pltpu.CompilerParams(vmem_limit_bytes=16 * 2**20),
    )(*parts)
    return pre.reshape(all_rows, 1, columns), scores


def solution(mesh):
    return jax.shard_map(
        functools.partial(on_device, mesh.shape["ex"], mesh.shape["mat"]),
        mesh=mesh,
        in_specs=(P(("ex", "mat"), None, None), P("mat", None, None), P("ex", "mat", None)),
        out_specs=(P("ex", "mat", None), P("mat", "ex")),
        check_vma=False,
    )
```

```python
import functools

import jax
import jax.numpy as jnp
from jax import lax
from jax.experimental import pallas as pl
from jax.experimental.pallas import tpu as pltpu
from jax.sharding import PartitionSpec as P

MESH = pl.DeviceIdType.MESH
F32, BF16 = jnp.float32, jnp.bfloat16
GROUPS = 4
LAST = GROUPS - 1
ZS = 8
TILE = 512
WIDE = 1024

PEERS = (
    (0, 4), (1, 4), (0, 3), (0, 5), (1, 3), (1, 5), (0, 2), (0, 6),
    (1, 2), (1, 6), (0, 1), (0, 7), (1, 1), (1, 7), (1, 0),
)
Z_PEERS = (4, 3, 5, 2, 6, 1, 7)
SAME = tuple(i for i, (dx, dz) in enumerate(PEERS) if dz % 2 == 0)
OTHER = tuple(i for i, (dx, dz) in enumerate(PEERS) if dz % 2 == 1)


def kernel(
    n_ex,
    n_mat,
    train_ref,
    hess_ref,
    query_ref,
    pre_ref,
    own,
    own_last,
    z_in,
    last_in,
    staged,
    outgoing,
    arrived,
    hess,
    queries,
    carried,
    terms,
    x_out,
    x_in,
    z_out,
    last_out,
    last_terms_out,
    load_sem,
    hess_sem,
    query_load_sem,
    send_sem,
    recv_sem,
    query_send_sem,
    query_recv_sem,
    x_send_sem,
    x_recv_sem,
    z_send_sem,
    z_recv_sem,
    term_send_sem,
    term_recv_sem,
):
    me = lax.axis_index("mat")
    my_ex = lax.axis_index("ex")
    side, place = me // ZS, lax.rem(me, ZS)
    z_at = [place] + [lax.rem(place + k, ZS) for k in range(1, ZS)]
    x_at = [side, 1 - side]
    peers = [x_at[dx] * ZS + z_at[dz] for dx, dz in PEERS]
    n_peers = len(PEERS)

    group_rows = train_ref.shape[0] // GROUPS
    part = group_rows // n_mat
    columns = train_ref.shape[1]
    n_queries = queries.shape[0]
    share = n_queries // n_mat
    half = n_queries // 2
    ex_share = query_ref.shape[0]

    parity = lax.rem(place, 2)
    mine = pl.ds(pl.multiple_of(me * part, part), part)
    slot = parity * (n_mat // 2) + side * (ZS // 2) + place // 2
    my_slot = pl.ds(pl.multiple_of(slot * part, part), part)
    my_queries = pl.ds(pl.multiple_of(my_ex * ex_share, ex_share), ex_share)
    my_half = pl.ds(pl.multiple_of(side * half, half), half)
    other_half = pl.ds(pl.multiple_of((1 - side) * half, half), half)
    my_terms = pl.ds(pl.multiple_of(me * share, share), share)

    def load(g):
        rows = pl.ds(g * group_rows, group_rows)
        return pltpu.make_async_copy(train_ref.at[rows], staged.at[g], load_sem.at[g])

    query_load = pltpu.make_async_copy(query_ref, queries.at[my_queries], query_load_sem)
    hess_load = pltpu.make_async_copy(hess_ref, hess, hess_sem)

    quarter = group_rows // 4
    for k in range(4):
        rows = pl.ds(k * quarter, quarter)
        pltpu.make_async_copy(train_ref.at[rows], staged.at[0, rows], load_sem.at[0]).start()
    query_load.start()
    barrier = pltpu.get_barrier_semaphore()
    for to in peers:
        pl.semaphore_signal(barrier, inc=1, device_id={"mat": to}, device_id_type=MESH)
    core = lax.rem(my_ex, 2)
    ex_peers = [my_ex + 1 - 2 * core] + [lax.rem(my_ex + k, n_ex) for k in range(2, n_ex, 2)]
    for to in ex_peers:
        pl.semaphore_signal(barrier, inc=1, device_id={"ex": to}, device_id_type=MESH)

    out_row = lax.broadcasted_iota(jnp.int32, (group_rows, group_rows), 0)
    in_row = lax.broadcasted_iota(jnp.int32, (group_rows, group_rows), 1)
    regroup = jnp.where(
        in_row == lax.rem(out_row, part) * n_mat + out_row // part, 1.0, 0.0
    ).astype(BF16)

    def regroup_rows(g):
        load(g).wait()
        for c in range(columns // TILE):
            cols = pl.ds(c * TILE, TILE)
            outgoing[g, :, cols] = jnp.dot(
                regroup, staged[g, :, cols], preferred_element_type=F32
            ).astype(BF16)
        arrived[g, my_slot, :] = outgoing[g, mine, :]

    def to_mat(src, dst, sent, received, device):
        return pltpu.make_async_remote_copy(
            src_ref=src,
            dst_ref=dst,
            send_sem=sent,
            recv_sem=received,
            device_id={"mat": device},
            device_id_type=MESH,
        )

    def send(g, i):
        rows = pl.ds(pl.multiple_of(peers[i] * part, part), part)
        k = g + 1 if g == LAST and i in OTHER else g
        return to_mat(
            outgoing.at[g, rows], arrived.at[g, my_slot], send_sem.at[k], recv_sem.at[k], peers[i]
        )

    def all_sends(k):
        count = n_peers if k < LAST else len(SAME) if k == LAST else len(OTHER)
        rows = pl.ds(0, part * count)
        g = min(k, LAST)
        return to_mat(
            outgoing.at[g, rows], arrived.at[g, rows], send_sem.at[k], recv_sem.at[k], peers[0]
        )

    def to_ex(rows, sem, device):
        return pltpu.make_async_remote_copy(
            src_ref=queries.at[rows],
            dst_ref=queries.at[rows],
            send_sem=query_send_sem.at[sem],
            recv_sem=query_recv_sem.at[sem],
            device_id={"ex": device},
            device_id_type=MESH,
        )

    pair_rows = 2 * ex_share
    my_pair = pl.ds(pl.multiple_of(my_ex // 2 * pair_rows, pair_rows), pair_rows)
    to_core = to_ex(my_queries, 0, ex_peers[0])
    all_pairs = to_ex(pl.ds(0, pair_rows * (len(ex_peers) - 1)), 1, ex_peers[1])

    def x_copy(g):
        return to_mat(x_out.at[g], x_in.at[g], x_send_sem.at[g], x_recv_sem.at[g], peers[-1])

    def z_copy(g, i):
        to = z_at[Z_PEERS[i]]
        return to_mat(
            z_out.at[g, pl.ds(pl.multiple_of(to * share, share), share)],
            z_in.at[g, i],
            z_send_sem.at[g],
            z_recv_sem.at[g],
            side * ZS + to,
        )

    def all_z(g):
        slots = pl.ds(0, len(Z_PEERS))
        return to_mat(
            z_in.at[g, slots], z_in.at[g, slots], z_send_sem.at[g], z_recv_sem.at[g], peers[0]
        )

    def term_copy(h, i):
        rows = pl.ds(pl.multiple_of(peers[i] * share, share), share)
        to = parity if h == 0 else 1 - parity
        return to_mat(
            last_out.at[h, rows], last_in.at[i, to], term_send_sem, term_recv_sem, peers[i]
        )

    all_terms = to_mat(last_in, last_in, term_send_sem, term_recv_sem, peers[0])

    def multiply(g):
        def tile(c, carry):
            cols = pl.ds(pl.multiple_of(c * WIDE, WIDE), WIDE)
            product = jnp.dot(arrived[g], hess[:, cols], preferred_element_type=F32)
            product = product.astype(BF16).reshape(n_mat, part, WIDE)
            for at in range(n_mat):
                odd, x, z = at // (n_mat // 2), at // (ZS // 2) % 2, at % (ZS // 2)
                pre_ref[x * ZS + 2 * z + odd, pl.ds(g * part, part), cols] = product[at]
            return carry

        lax.fori_loop(0, columns // WIDE, tile, 0)

    def scores_of(left, rows):
        return lax.dot_general(left, rows, (((1,), (1,)), ((), ())), preferred_element_type=F32)

    def start_terms(g):
        rows = pre_ref[:, pl.ds(g * part, part), :].reshape(group_rows, columns)
        terms[...] = scores_of(queries[...], rows)
        x_out[g] = terms[other_half, :].astype(BF16)
        x_copy(g).start()

    def pass_terms(g):
        x_copy(g).wait_recv()
        terms[my_half, :] = terms[my_half, :] + x_in[g].astype(F32)
        z_out[g] = terms[my_half, :].astype(BF16)
        for i in range(len(Z_PEERS)):
            z_copy(g, i).start()
        own[g] = terms[my_terms, :]

    regroup_rows(0)
    query_load.wait()
    pl.semaphore_wait(barrier, len(peers) + len(ex_peers))
    to_core.start()
    for i in range(n_peers):
        send(0, i).start()
    for g in range(1, GROUPS):
        load(g).start()
    hess_load.start()
    to_core.wait_recv()
    for to in ex_peers[1:]:
        to_ex(my_pair, 1, to).start()
    regroup_rows(1)
    for i in range(n_peers):
        send(1, i).start()
    for g in range(2, GROUPS):
        regroup_rows(g)

    def last_terms(h):
        at = parity if h == 0 else 1 - parity
        rows = pl.ds(pl.multiple_of(at * (group_rows // 2), group_rows // 2), group_rows // 2)
        product = scores_of(carried[...], arrived[LAST, rows, :])
        last_terms_out[...] = product
        last_out[h] = product.astype(BF16)
        for i in range(n_peers):
            term_copy(h, i).start()
        own_last[at] = last_terms_out[my_terms, :]

    for g in range(LAST):
        all_sends(g).wait_recv()
        for i in range(n_peers) if g + 2 <= LAST else ():
            send(g + 2, i).start()
        if g == 0:
            all_pairs.wait_recv()
            hess_load.wait()
        multiply(g)
        if g > 0:
            pass_terms(g - 1)
        start_terms(g)
        if g == 0:

            def carry_back(c, carry):
                cols = pl.ds(pl.multiple_of(c * TILE, TILE), TILE)
                carried[:, cols] = scores_of(queries[...], hess[cols, :]).astype(BF16)
                return carry

            lax.fori_loop(0, columns // TILE, carry_back, 0)
        else:
            all_sends(g - 1).wait_send()

    all_sends(LAST).wait_recv()
    last_terms(0)
    pass_terms(LAST - 1)
    all_sends(LAST + 1).wait_recv()
    last_terms(1)
    multiply(LAST)

    to_core.wait_send()
    all_pairs.wait_send()
    for k in range(LAST - 1, LAST + 2):
        all_sends(k).wait_send()
    for g in range(LAST):
        x_copy(g).wait_send()
        all_z(g).wait_send()
        all_z(g).wait_recv()
    all_terms.wait_send()
    all_terms.wait_recv()


def finish(pre_ref, own, own_last, z_in, last_in, out_ref, scores_ref, scores, out_sem, scores_sem):
    n_mat = pre_ref.shape[0]
    pieces = out_sem.shape[0]
    step = n_mat // pieces
    part = own.shape[2] // n_mat

    def out_copy(k):
        mats = pl.ds(k * step, step)
        return pltpu.make_async_copy(pre_ref.at[mats], out_ref.at[mats], out_sem.at[k])

    for k in range(pieces):
        out_copy(k).start()
    totals = []
    for g in range(LAST):
        total = own[g]
        for i in range(len(Z_PEERS)):
            total += z_in[g, i].astype(F32)
        totals += [total[:, :128], total[:, 128:]]
    for h in range(2):
        total = own_last[h]
        for i in range(len(PEERS)):
            total += last_in[i, h].astype(F32)
        totals.append(total)
    lane = lax.broadcasted_iota(jnp.int32, (own.shape[1], 128), 1)
    for j in range(n_mat // 2):
        tile = jnp.zeros(lane.shape, F32)
        for s in range(2):
            mat = 2 * j + s
            for g in range(GROUPS):
                x, z = mat // ZS, mat % ZS
                slot = mat if g < LAST else z % 2 * (n_mat // 2) + x * (ZS // 2) + z // 2
                at, half = (slot * part) % 128, slot * part // 128
                to = (s * GROUPS + g) * part
                moved = pltpu.roll(totals[2 * g + half], (to - at) % 128, 1)
                tile = jnp.where((lane >= to) & (lane < to + part), moved, tile)
        scores[:, j * 128 : j * 128 + 128] = tile
    scores_copy = pltpu.make_async_copy(scores, scores_ref, scores_sem)
    scores_copy.start()
    for k in range(pieces):
        out_copy(k).wait()
    scores_copy.wait()


def in_hbm(array):
    return pltpu.with_memory_space_constraint(array, pltpu.HBM)


def on_device(n_ex, n_mat, train_grads, inverse_hessian, query_grads):
    rows, mats, columns = train_grads.shape
    all_rows = rows * mats
    group_rows = all_rows // GROUPS
    n_queries = query_grads.shape[0] * n_ex
    share = n_queries // n_mat
    dma = pltpu.SemaphoreType.DMA
    in_vmem = pl.BlockSpec(memory_space=pltpu.VMEM)
    anywhere = pl.BlockSpec(memory_space=pl.ANY)
    parts = pl.pallas_call(
        functools.partial(kernel, n_ex, n_mat),
        name="influence",
        out_shape=(
            pltpu.VMEM((mats, rows, columns), BF16),
            pltpu.VMEM((LAST, share, group_rows), F32),
            pltpu.VMEM((2, share, group_rows // 2), F32),
            pltpu.VMEM((LAST, len(Z_PEERS), share, group_rows), BF16),
            pltpu.VMEM((len(PEERS), 2, share, group_rows // 2), BF16),
        ),
        in_specs=[anywhere] * 3,
        out_specs=(in_vmem,) * 5,
        scratch_shapes=[
            pltpu.VMEM((GROUPS, group_rows, columns), BF16),
            pltpu.VMEM((GROUPS, group_rows, columns), BF16),
            pltpu.VMEM((GROUPS, group_rows, columns), BF16),
            pltpu.VMEM((columns, columns), BF16),
            pltpu.VMEM((n_queries, columns), BF16),
            pltpu.VMEM((n_queries, columns), BF16),
            pltpu.VMEM((n_queries, group_rows), F32),
            pltpu.VMEM((LAST, n_queries // 2, group_rows), BF16),
            pltpu.VMEM((LAST, n_queries // 2, group_rows), BF16),
            pltpu.VMEM((LAST, n_queries // 2, group_rows), BF16),
            pltpu.VMEM((2, n_queries, group_rows // 2), BF16),
            pltpu.VMEM((n_queries, group_rows // 2), F32),
            dma((GROUPS,)),
            dma,
            dma,
            dma((GROUPS + 1,)),
            dma((GROUPS + 1,)),
            dma((2,)),
            dma((2,)),
            dma((LAST,)),
            dma((LAST,)),
            dma((LAST,)),
            dma((LAST,)),
            dma,
            dma,
        ],
        compiler_params=pltpu.CompilerParams(
            collective_id=0, has_side_effects=True, vmem_limit_bytes=40 * 2**20
        ),
        cost_estimate=pl.CostEstimate(
            flops=2 * all_rows * columns * (columns + n_queries),
            bytes_accessed=2 * columns * (2 * all_rows + columns),
            transcendentals=0,
        ),
    )(
        in_hbm(train_grads.reshape(all_rows, columns)),
        in_hbm(inverse_hessian.reshape(columns, columns)),
        in_hbm(query_grads.reshape(query_grads.shape[0], columns)),
    )
    pre, scores = pl.pallas_call(
        finish,
        name="write_out",
        out_shape=(
            pltpu.HBM((mats, rows, columns), BF16),
            pltpu.HBM((share, all_rows), F32),
        ),
        in_specs=[in_vmem] * 5,
        out_specs=(anywhere,) * 2,
        scratch_shapes=[pltpu.VMEM((share, all_rows), F32), dma((4,)), dma],
        compiler_params=pltpu.CompilerParams(vmem_limit_bytes=16 * 2**20),
    )(*parts)
    return pre.reshape(all_rows, 1, columns), scores


def solution(mesh):
    return jax.shard_map(
        functools.partial(on_device, mesh.shape["ex"], mesh.shape["mat"]),
        mesh=mesh,
        in_specs=(P(("ex", "mat"), None, None), P("mat", None, None), P("ex", "mat", None)),
        out_specs=(P("ex", "mat", None), P("mat", "ex")),
        check_vma=False,
    )
```

```python
import functools

import jax
import jax.numpy as jnp
from jax import lax
from jax.experimental import pallas as pl
from jax.experimental.pallas import tpu as pltpu
from jax.sharding import PartitionSpec as P

MESH = pl.DeviceIdType.MESH
F32, BF16 = jnp.float32, jnp.bfloat16
GROUPS = 4
LAST = GROUPS - 1
ZS = 8
TILE = 512
WIDE = 2048

PEERS = (
    (0, 4), (1, 4), (0, 3), (0, 5), (1, 3), (1, 5), (0, 2), (0, 6),
    (1, 2), (1, 6), (0, 1), (0, 7), (1, 1), (1, 7), (1, 0),
)
Z_PEERS = (4, 3, 5, 2, 6, 1, 7)
SAME = tuple(i for i, (dx, dz) in enumerate(PEERS) if dz % 2 == 0)
OTHER = tuple(i for i, (dx, dz) in enumerate(PEERS) if dz % 2 == 1)


def kernel(
    n_ex,
    n_mat,
    train_ref,
    hess_ref,
    query_ref,
    pre_ref,
    own,
    own_last,
    z_in,
    last_in,
    staged,
    outgoing,
    arrived,
    hess,
    queries,
    carried,
    terms,
    x_out,
    x_in,
    z_out,
    last_out,
    last_terms_out,
    load_sem,
    hess_sem,
    query_load_sem,
    send_sem,
    recv_sem,
    query_send_sem,
    query_recv_sem,
    x_send_sem,
    x_recv_sem,
    z_send_sem,
    z_recv_sem,
    term_send_sem,
    term_recv_sem,
):
    me = lax.axis_index("mat")
    my_ex = lax.axis_index("ex")
    side, place = me // ZS, lax.rem(me, ZS)
    z_at = [place] + [lax.rem(place + k, ZS) for k in range(1, ZS)]
    x_at = [side, 1 - side]
    peers = [x_at[dx] * ZS + z_at[dz] for dx, dz in PEERS]
    n_peers = len(PEERS)

    group_rows = train_ref.shape[0] // GROUPS
    part = group_rows // n_mat
    columns = train_ref.shape[1]
    n_queries = queries.shape[0]
    share = n_queries // n_mat
    half = n_queries // 2
    ex_share = query_ref.shape[0]

    parity = lax.rem(place, 2)
    mine = pl.ds(pl.multiple_of(me * part, part), part)
    slot = parity * (n_mat // 2) + side * (ZS // 2) + place // 2
    my_slot = pl.ds(pl.multiple_of(slot * part, part), part)
    my_queries = pl.ds(pl.multiple_of(my_ex * ex_share, ex_share), ex_share)
    my_half = pl.ds(pl.multiple_of(side * half, half), half)
    other_half = pl.ds(pl.multiple_of((1 - side) * half, half), half)
    my_terms = pl.ds(pl.multiple_of(me * share, share), share)

    def load(g):
        rows = pl.ds(g * group_rows, group_rows)
        return pltpu.make_async_copy(train_ref.at[rows], staged.at[g], load_sem.at[g])

    query_load = pltpu.make_async_copy(query_ref, queries.at[my_queries], query_load_sem)
    hess_load = pltpu.make_async_copy(hess_ref, hess, hess_sem)

    quarter = group_rows // 4
    for k in range(4):
        rows = pl.ds(k * quarter, quarter)
        pltpu.make_async_copy(train_ref.at[rows], staged.at[0, rows], load_sem.at[0]).start()
    query_load.start()
    barrier = pltpu.get_barrier_semaphore()
    for to in peers:
        pl.semaphore_signal(barrier, inc=1, device_id={"mat": to}, device_id_type=MESH)
    core = lax.rem(my_ex, 2)
    ex_peers = [my_ex + 1 - 2 * core] + [lax.rem(my_ex + k, n_ex) for k in range(2, n_ex, 2)]
    for to in ex_peers:
        pl.semaphore_signal(barrier, inc=1, device_id={"ex": to}, device_id_type=MESH)

    out_row = lax.broadcasted_iota(jnp.int32, (group_rows, group_rows), 0)
    in_row = lax.broadcasted_iota(jnp.int32, (group_rows, group_rows), 1)
    regroup = jnp.where(
        in_row == lax.rem(out_row, part) * n_mat + out_row // part, 1.0, 0.0
    ).astype(BF16)

    def regroup_rows(g):
        load(g).wait()
        for c in range(columns // TILE):
            cols = pl.ds(c * TILE, TILE)
            outgoing[g, :, cols] = jnp.dot(
                regroup, staged[g, :, cols], preferred_element_type=F32
            ).astype(BF16)
        arrived[g, my_slot, :] = outgoing[g, mine, :]

    def to_mat(src, dst, sent, received, device):
        return pltpu.make_async_remote_copy(
            src_ref=src,
            dst_ref=dst,
            send_sem=sent,
            recv_sem=received,
            device_id={"mat": device},
            device_id_type=MESH,
        )

    def send(g, i):
        rows = pl.ds(pl.multiple_of(peers[i] * part, part), part)
        k = g + 1 if g == LAST and i in OTHER else g
        return to_mat(
            outgoing.at[g, rows], arrived.at[g, my_slot], send_sem.at[k], recv_sem.at[k], peers[i]
        )

    def all_sends(k):
        count = n_peers if k < LAST else len(SAME) if k == LAST else len(OTHER)
        rows = pl.ds(0, part * count)
        g = min(k, LAST)
        return to_mat(
            outgoing.at[g, rows], arrived.at[g, rows], send_sem.at[k], recv_sem.at[k], peers[0]
        )

    def to_ex(rows, sem, device):
        return pltpu.make_async_remote_copy(
            src_ref=queries.at[rows],
            dst_ref=queries.at[rows],
            send_sem=query_send_sem.at[sem],
            recv_sem=query_recv_sem.at[sem],
            device_id={"ex": device},
            device_id_type=MESH,
        )

    pair_rows = 2 * ex_share
    my_pair = pl.ds(pl.multiple_of(my_ex // 2 * pair_rows, pair_rows), pair_rows)
    to_core = to_ex(my_queries, 0, ex_peers[0])
    all_pairs = to_ex(pl.ds(0, pair_rows * (len(ex_peers) - 1)), 1, ex_peers[1])

    def x_copy(g):
        return to_mat(x_out.at[g], x_in.at[g], x_send_sem.at[g], x_recv_sem.at[g], peers[-1])

    def z_copy(g, i):
        to = z_at[Z_PEERS[i]]
        return to_mat(
            z_out.at[g, pl.ds(pl.multiple_of(to * share, share), share)],
            z_in.at[g, i],
            z_send_sem.at[g],
            z_recv_sem.at[g],
            side * ZS + to,
        )

    def all_z(g):
        slots = pl.ds(0, len(Z_PEERS))
        return to_mat(
            z_in.at[g, slots], z_in.at[g, slots], z_send_sem.at[g], z_recv_sem.at[g], peers[0]
        )

    def term_copy(h, i):
        rows = pl.ds(pl.multiple_of(peers[i] * share, share), share)
        to = parity if h == 0 else 1 - parity
        return to_mat(
            last_out.at[h, rows], last_in.at[i, to], term_send_sem, term_recv_sem, peers[i]
        )

    all_terms = to_mat(last_in, last_in, term_send_sem, term_recv_sem, peers[0])

    def multiply(g):
        def tile(c, carry):
            cols = pl.ds(pl.multiple_of(c * WIDE, WIDE), WIDE)
            product = jnp.dot(arrived[g], hess[:, cols], preferred_element_type=F32)
            product = product.astype(BF16).reshape(n_mat, part, WIDE)
            for at in range(n_mat):
                odd, x, z = at // (n_mat // 2), at // (ZS // 2) % 2, at % (ZS // 2)
                pre_ref[x * ZS + 2 * z + odd, pl.ds(g * part, part), cols] = product[at]
            return carry

        lax.fori_loop(0, columns // WIDE, tile, 0)

    def scores_of(left, rows):
        return lax.dot_general(left, rows, (((1,), (1,)), ((), ())), preferred_element_type=F32)

    def start_terms(g):
        rows = pre_ref[:, pl.ds(g * part, part), :].reshape(group_rows, columns)
        terms[...] = scores_of(queries[...], rows)
        x_out[g] = terms[other_half, :].astype(BF16)
        x_copy(g).start()

    def pass_terms(g):
        x_copy(g).wait_recv()
        terms[my_half, :] = terms[my_half, :] + x_in[g].astype(F32)
        z_out[g] = terms[my_half, :].astype(BF16)
        for i in range(len(Z_PEERS)):
            z_copy(g, i).start()
        own[g] = terms[my_terms, :]

    regroup_rows(0)
    query_load.wait()
    pl.semaphore_wait(barrier, len(peers) + len(ex_peers))
    to_core.start()
    for i in range(n_peers):
        send(0, i).start()
    for g in range(1, GROUPS):
        load(g).start()
    hess_load.start()
    to_core.wait_recv()
    for to in ex_peers[1:]:
        to_ex(my_pair, 1, to).start()
    regroup_rows(1)
    for i in range(n_peers):
        send(1, i).start()
    for g in range(2, GROUPS):
        regroup_rows(g)

    def last_terms(h):
        at = parity if h == 0 else 1 - parity
        rows = pl.ds(pl.multiple_of(at * (group_rows // 2), group_rows // 2), group_rows // 2)
        product = scores_of(carried[...], arrived[LAST, rows, :])
        last_terms_out[...] = product
        last_out[h] = product.astype(BF16)
        for i in range(n_peers):
            term_copy(h, i).start()
        own_last[at] = last_terms_out[my_terms, :]

    for g in range(LAST):
        all_sends(g).wait_recv()
        for i in range(n_peers) if g + 2 <= LAST else ():
            send(g + 2, i).start()
        if g == 0:
            all_pairs.wait_recv()
            hess_load.wait()
        multiply(g)
        if g > 0:
            pass_terms(g - 1)
        start_terms(g)
        if g == 0:

            def carry_back(c, carry):
                cols = pl.ds(pl.multiple_of(c * TILE, TILE), TILE)
                carried[:, cols] = scores_of(queries[...], hess[cols, :]).astype(BF16)
                return carry

            lax.fori_loop(0, columns // TILE, carry_back, 0)
        else:
            all_sends(g - 1).wait_send()

    all_sends(LAST).wait_recv()
    last_terms(0)
    all_sends(LAST + 1).wait_recv()
    last_terms(1)
    pass_terms(LAST - 1)
    multiply(LAST)

    to_core.wait_send()
    all_pairs.wait_send()
    for k in range(LAST - 1, LAST + 2):
        all_sends(k).wait_send()
    for g in range(LAST):
        x_copy(g).wait_send()
        all_z(g).wait_send()
        all_z(g).wait_recv()
    all_terms.wait_send()
    all_terms.wait_recv()


def finish(pre_ref, own, own_last, z_in, last_in, out_ref, scores_ref, scores, out_sem, scores_sem):
    n_mat = pre_ref.shape[0]
    pieces = out_sem.shape[0]
    step = n_mat // pieces
    part = own.shape[2] // n_mat

    def out_copy(k):
        mats = pl.ds(k * step, step)
        return pltpu.make_async_copy(pre_ref.at[mats], out_ref.at[mats], out_sem.at[k])

    for k in range(pieces):
        out_copy(k).start()
    totals = []
    for g in range(LAST):
        total = own[g]
        for i in range(len(Z_PEERS)):
            total += z_in[g, i].astype(F32)
        totals += [total[:, :128], total[:, 128:]]
    for h in range(2):
        total = own_last[h]
        for i in range(len(PEERS)):
            total += last_in[i, h].astype(F32)
        totals.append(total)
    lane = lax.broadcasted_iota(jnp.int32, (own.shape[1], 128), 1)
    for j in range(n_mat // 2):
        tile = jnp.zeros(lane.shape, F32)
        for s in range(2):
            mat = 2 * j + s
            for g in range(GROUPS):
                x, z = mat // ZS, mat % ZS
                slot = mat if g < LAST else z % 2 * (n_mat // 2) + x * (ZS // 2) + z // 2
                at, half = (slot * part) % 128, slot * part // 128
                to = (s * GROUPS + g) * part
                moved = pltpu.roll(totals[2 * g + half], (to - at) % 128, 1)
                tile = jnp.where((lane >= to) & (lane < to + part), moved, tile)
        scores[:, j * 128 : j * 128 + 128] = tile
    scores_copy = pltpu.make_async_copy(scores, scores_ref, scores_sem)
    scores_copy.start()
    for k in range(pieces):
        out_copy(k).wait()
    scores_copy.wait()


def in_hbm(array):
    return pltpu.with_memory_space_constraint(array, pltpu.HBM)


def on_device(n_ex, n_mat, train_grads, inverse_hessian, query_grads):
    rows, mats, columns = train_grads.shape
    all_rows = rows * mats
    group_rows = all_rows // GROUPS
    n_queries = query_grads.shape[0] * n_ex
    share = n_queries // n_mat
    dma = pltpu.SemaphoreType.DMA
    in_vmem = pl.BlockSpec(memory_space=pltpu.VMEM)
    anywhere = pl.BlockSpec(memory_space=pl.ANY)
    parts = pl.pallas_call(
        functools.partial(kernel, n_ex, n_mat),
        name="influence",
        out_shape=(
            pltpu.VMEM((mats, rows, columns), BF16),
            pltpu.VMEM((LAST, share, group_rows), F32),
            pltpu.VMEM((2, share, group_rows // 2), F32),
            pltpu.VMEM((LAST, len(Z_PEERS), share, group_rows), BF16),
            pltpu.VMEM((len(PEERS), 2, share, group_rows // 2), BF16),
        ),
        in_specs=[anywhere] * 3,
        out_specs=(in_vmem,) * 5,
        scratch_shapes=[
            pltpu.VMEM((GROUPS, group_rows, columns), BF16),
            pltpu.VMEM((GROUPS, group_rows, columns), BF16),
            pltpu.VMEM((GROUPS, group_rows, columns), BF16),
            pltpu.VMEM((columns, columns), BF16),
            pltpu.VMEM((n_queries, columns), BF16),
            pltpu.VMEM((n_queries, columns), BF16),
            pltpu.VMEM((n_queries, group_rows), F32),
            pltpu.VMEM((LAST, n_queries // 2, group_rows), BF16),
            pltpu.VMEM((LAST, n_queries // 2, group_rows), BF16),
            pltpu.VMEM((LAST, n_queries // 2, group_rows), BF16),
            pltpu.VMEM((2, n_queries, group_rows // 2), BF16),
            pltpu.VMEM((n_queries, group_rows // 2), F32),
            dma((GROUPS,)),
            dma,
            dma,
            dma((GROUPS + 1,)),
            dma((GROUPS + 1,)),
            dma((2,)),
            dma((2,)),
            dma((LAST,)),
            dma((LAST,)),
            dma((LAST,)),
            dma((LAST,)),
            dma,
            dma,
        ],
        compiler_params=pltpu.CompilerParams(
            collective_id=0, has_side_effects=True, vmem_limit_bytes=40 * 2**20
        ),
        cost_estimate=pl.CostEstimate(
            flops=2 * all_rows * columns * (columns + n_queries),
            bytes_accessed=2 * columns * (2 * all_rows + columns),
            transcendentals=0,
        ),
    )(
        in_hbm(train_grads.reshape(all_rows, columns)),
        in_hbm(inverse_hessian.reshape(columns, columns)),
        in_hbm(query_grads.reshape(query_grads.shape[0], columns)),
    )
    pre, scores = pl.pallas_call(
        finish,
        name="write_out",
        out_shape=(
            pltpu.HBM((mats, rows, columns), BF16),
            pltpu.HBM((share, all_rows), F32),
        ),
        in_specs=[in_vmem] * 5,
        out_specs=(anywhere,) * 2,
        scratch_shapes=[pltpu.VMEM((share, all_rows), F32), dma((4,)), dma],
        compiler_params=pltpu.CompilerParams(vmem_limit_bytes=16 * 2**20),
    )(*parts)
    return pre.reshape(all_rows, 1, columns), scores


def solution(mesh):
    return jax.shard_map(
        functools.partial(on_device, mesh.shape["ex"], mesh.shape["mat"]),
        mesh=mesh,
        in_specs=(P(("ex", "mat"), None, None), P("mat", None, None), P("ex", "mat", None)),
        out_specs=(P("ex", "mat", None), P("mat", "ex")),
        check_vma=False,
    )
```

```python
import functools

import jax
import jax.numpy as jnp
from jax import lax
from jax.experimental import pallas as pl
from jax.experimental.pallas import tpu as pltpu
from jax.sharding import PartitionSpec as P

MESH = pl.DeviceIdType.MESH
F32, BF16 = jnp.float32, jnp.bfloat16
GROUPS = 4
LAST = GROUPS - 1
ZS = 8
TILE = 512
WIDE = 1024

PEERS = (
    (0, 4), (1, 4), (0, 3), (0, 5), (1, 3), (1, 5), (0, 2), (0, 6),
    (1, 2), (1, 6), (0, 1), (0, 7), (1, 1), (1, 7), (1, 0),
)
Z_PEERS = (4, 3, 5, 2, 6, 1, 7)
SAME = tuple(i for i, (dx, dz) in enumerate(PEERS) if dz % 2 == 0)
OTHER = tuple(i for i, (dx, dz) in enumerate(PEERS) if dz % 2 == 1)


def kernel(
    n_ex,
    n_mat,
    train_ref,
    hess_ref,
    query_ref,
    pre_ref,
    own,
    own_last,
    z_in,
    last_in,
    staged,
    outgoing,
    arrived,
    hess,
    queries,
    carried,
    terms,
    x_out,
    x_in,
    z_out,
    last_out,
    last_terms_out,
    load_sem,
    hess_sem,
    query_load_sem,
    send_sem,
    recv_sem,
    query_send_sem,
    query_recv_sem,
    x_send_sem,
    x_recv_sem,
    z_send_sem,
    z_recv_sem,
    term_send_sem,
    term_recv_sem,
):
    me = lax.axis_index("mat")
    my_ex = lax.axis_index("ex")
    side, place = me // ZS, lax.rem(me, ZS)
    z_at = [place] + [lax.rem(place + k, ZS) for k in range(1, ZS)]
    x_at = [side, 1 - side]
    peers = [x_at[dx] * ZS + z_at[dz] for dx, dz in PEERS]
    n_peers = len(PEERS)

    group_rows = train_ref.shape[0] // GROUPS
    part = group_rows // n_mat
    columns = train_ref.shape[1]
    n_queries = queries.shape[0]
    share = n_queries // n_mat
    half = n_queries // 2
    ex_share = query_ref.shape[0]

    parity = lax.rem(place, 2)
    mine = pl.ds(pl.multiple_of(me * part, part), part)
    slot = parity * (n_mat // 2) + side * (ZS // 2) + place // 2
    my_slot = pl.ds(pl.multiple_of(slot * part, part), part)
    my_queries = pl.ds(pl.multiple_of(my_ex * ex_share, ex_share), ex_share)
    my_half = pl.ds(pl.multiple_of(side * half, half), half)
    other_half = pl.ds(pl.multiple_of((1 - side) * half, half), half)
    my_terms = pl.ds(pl.multiple_of(me * share, share), share)

    def load(g):
        rows = pl.ds(g * group_rows, group_rows)
        return pltpu.make_async_copy(train_ref.at[rows], staged.at[g], load_sem.at[g])

    query_load = pltpu.make_async_copy(query_ref, queries.at[my_queries], query_load_sem)
    hess_load = pltpu.make_async_copy(hess_ref, hess, hess_sem)

    quarter = group_rows // 4
    for k in range(4):
        rows = pl.ds(k * quarter, quarter)
        pltpu.make_async_copy(train_ref.at[rows], staged.at[0, rows], load_sem.at[0]).start()
    query_load.start()
    barrier = pltpu.get_barrier_semaphore()
    for to in peers:
        pl.semaphore_signal(barrier, inc=1, device_id={"mat": to}, device_id_type=MESH)
    core = lax.rem(my_ex, 2)
    ex_peers = [my_ex + 1 - 2 * core] + [lax.rem(my_ex + k, n_ex) for k in range(2, n_ex, 2)]
    for to in ex_peers:
        pl.semaphore_signal(barrier, inc=1, device_id={"ex": to}, device_id_type=MESH)

    out_row = lax.broadcasted_iota(jnp.int32, (group_rows, group_rows), 0)
    in_row = lax.broadcasted_iota(jnp.int32, (group_rows, group_rows), 1)
    regroup = jnp.where(
        in_row == lax.rem(out_row, part) * n_mat + out_row // part, 1.0, 0.0
    ).astype(BF16)

    def regroup_rows(g):
        load(g).wait()
        for c in range(columns // TILE):
            cols = pl.ds(c * TILE, TILE)
            outgoing[g, :, cols] = jnp.dot(
                regroup, staged[g, :, cols], preferred_element_type=F32
            ).astype(BF16)
        arrived[g, my_slot, :] = outgoing[g, mine, :]

    def to_mat(src, dst, sent, received, device):
        return pltpu.make_async_remote_copy(
            src_ref=src,
            dst_ref=dst,
            send_sem=sent,
            recv_sem=received,
            device_id={"mat": device},
            device_id_type=MESH,
        )

    def send(g, i):
        rows = pl.ds(pl.multiple_of(peers[i] * part, part), part)
        k = g + 1 if g == LAST and i in OTHER else g
        return to_mat(
            outgoing.at[g, rows], arrived.at[g, my_slot], send_sem.at[k], recv_sem.at[k], peers[i]
        )

    def all_sends(k):
        count = n_peers if k < LAST else len(SAME) if k == LAST else len(OTHER)
        rows = pl.ds(0, part * count)
        g = min(k, LAST)
        return to_mat(
            outgoing.at[g, rows], arrived.at[g, rows], send_sem.at[k], recv_sem.at[k], peers[0]
        )

    def to_ex(rows, sem, device):
        return pltpu.make_async_remote_copy(
            src_ref=queries.at[rows],
            dst_ref=queries.at[rows],
            send_sem=query_send_sem.at[sem],
            recv_sem=query_recv_sem.at[sem],
            device_id={"ex": device},
            device_id_type=MESH,
        )

    pair_rows = 2 * ex_share
    my_pair = pl.ds(pl.multiple_of(my_ex // 2 * pair_rows, pair_rows), pair_rows)
    to_core = to_ex(my_queries, 0, ex_peers[0])
    all_pairs = to_ex(pl.ds(0, pair_rows * (len(ex_peers) - 1)), 1, ex_peers[1])

    def x_copy(g):
        return to_mat(x_out.at[g], x_in.at[g], x_send_sem.at[g], x_recv_sem.at[g], peers[-1])

    def z_copy(g, i):
        to = z_at[Z_PEERS[i]]
        return to_mat(
            z_out.at[g, pl.ds(pl.multiple_of(to * share, share), share)],
            z_in.at[g, i],
            z_send_sem.at[g],
            z_recv_sem.at[g],
            side * ZS + to,
        )

    def all_z(g):
        slots = pl.ds(0, len(Z_PEERS))
        return to_mat(
            z_in.at[g, slots], z_in.at[g, slots], z_send_sem.at[g], z_recv_sem.at[g], peers[0]
        )

    def term_copy(h, i):
        rows = pl.ds(pl.multiple_of(peers[i] * share, share), share)
        to = parity if h == 0 else 1 - parity
        return to_mat(
            last_out.at[h, rows], last_in.at[i, to], term_send_sem, term_recv_sem, peers[i]
        )

    all_terms = to_mat(last_in, last_in, term_send_sem, term_recv_sem, peers[0])

    def multiply(g):
        def tile(c, carry):
            cols = pl.ds(pl.multiple_of(c * WIDE, WIDE), WIDE)
            product = jnp.dot(arrived[g], hess[:, cols], preferred_element_type=F32)
            product = product.astype(BF16).reshape(n_mat, part, WIDE)
            for at in range(n_mat):
                odd, x, z = at // (n_mat // 2), at // (ZS // 2) % 2, at % (ZS // 2)
                pre_ref[x * ZS + 2 * z + odd, pl.ds(g * part, part), cols] = product[at]
            return carry

        lax.fori_loop(0, columns // WIDE, tile, 0)

    def scores_of(left, rows):
        return lax.dot_general(left, rows, (((1,), (1,)), ((), ())), preferred_element_type=F32)

    def start_terms(g):
        rows = pre_ref[:, pl.ds(g * part, part), :].reshape(group_rows, columns)
        terms[...] = scores_of(queries[...], rows)
        x_out[g] = terms[other_half, :].astype(BF16)
        x_copy(g).start()

    def pass_terms(g):
        x_copy(g).wait_recv()
        terms[my_half, :] = terms[my_half, :] + x_in[g].astype(F32)
        z_out[g] = terms[my_half, :].astype(BF16)
        for i in range(len(Z_PEERS)):
            z_copy(g, i).start()
        own[g] = terms[my_terms, :]

    regroup_rows(0)
    query_load.wait()
    pl.semaphore_wait(barrier, len(peers) + len(ex_peers))
    to_core.start()
    for i in range(n_peers):
        send(0, i).start()
    for g in range(1, GROUPS):
        load(g).start()
    hess_load.start()
    to_core.wait_recv()
    for to in ex_peers[1:]:
        to_ex(my_pair, 1, to).start()
    regroup_rows(1)
    for i in range(n_peers):
        send(1, i).start()
    for g in range(2, GROUPS):
        regroup_rows(g)

    def last_terms(h):
        at = parity if h == 0 else 1 - parity
        rows = pl.ds(pl.multiple_of(at * (group_rows // 2), group_rows // 2), group_rows // 2)
        product = scores_of(carried[...], arrived[LAST, rows, :])
        last_terms_out[...] = product
        last_out[h] = product.astype(BF16)
        for i in range(n_peers):
            term_copy(h, i).start()
        own_last[at] = last_terms_out[my_terms, :]

    for g in range(LAST):
        all_sends(g).wait_recv()
        for i in range(n_peers) if g + 2 <= LAST else ():
            send(g + 2, i).start()
        if g == 0:
            all_pairs.wait_recv()
            hess_load.wait()
        multiply(g)
        if g > 0:
            pass_terms(g - 1)
        start_terms(g)
        if g == 0:

            def carry_back(c, carry):
                cols = pl.ds(pl.multiple_of(c * TILE, TILE), TILE)
                carried[:, cols] = scores_of(queries[...], hess[cols, :]).astype(BF16)
                return carry

            lax.fori_loop(0, columns // TILE, carry_back, 0)
        else:
            all_sends(g - 1).wait_send()

    all_sends(LAST).wait_recv()
    last_terms(0)
    all_sends(LAST + 1).wait_recv()
    last_terms(1)
    pass_terms(LAST - 1)
    multiply(LAST)

    to_core.wait_send()
    all_pairs.wait_send()
    for k in range(LAST - 1, LAST + 2):
        all_sends(k).wait_send()
    for g in range(LAST):
        x_copy(g).wait_send()
        all_z(g).wait_send()
        all_z(g).wait_recv()
    all_terms.wait_send()
    all_terms.wait_recv()


def finish(pre_ref, own, own_last, z_in, last_in, out_ref, scores_ref, scores, out_sem, scores_sem):
    n_mat = pre_ref.shape[0]
    pieces = out_sem.shape[0]
    step = n_mat // pieces
    part = own.shape[2] // n_mat

    def out_copy(k):
        mats = pl.ds(k * step, step)
        return pltpu.make_async_copy(pre_ref.at[mats], out_ref.at[mats], out_sem.at[k])

    for k in range(pieces):
        out_copy(k).start()
    totals = []
    for g in range(LAST):
        total = own[g]
        for i in range(len(Z_PEERS)):
            total += z_in[g, i].astype(F32)
        totals += [total[:, :128], total[:, 128:]]
    for h in range(2):
        total = own_last[h]
        for i in range(len(PEERS)):
            total += last_in[i, h].astype(F32)
        totals.append(total)
    lane = lax.broadcasted_iota(jnp.int32, (own.shape[1], 128), 1)
    for j in range(n_mat // 2):
        tile = jnp.zeros(lane.shape, F32)
        for s in range(2):
            mat = 2 * j + s
            for g in range(GROUPS):
                x, z = mat // ZS, mat % ZS
                slot = mat if g < LAST else z % 2 * (n_mat // 2) + x * (ZS // 2) + z // 2
                at, half = (slot * part) % 128, slot * part // 128
                to = (s * GROUPS + g) * part
                moved = pltpu.roll(totals[2 * g + half], (to - at) % 128, 1)
                tile = jnp.where((lane >= to) & (lane < to + part), moved, tile)
        scores[:, j * 128 : j * 128 + 128] = tile
    scores_copy = pltpu.make_async_copy(scores, scores_ref, scores_sem)
    scores_copy.start()
    for k in range(pieces):
        out_copy(k).wait()
    scores_copy.wait()


def in_hbm(array):
    return pltpu.with_memory_space_constraint(array, pltpu.HBM)


def on_device(n_ex, n_mat, train_grads, inverse_hessian, query_grads):
    rows, mats, columns = train_grads.shape
    all_rows = rows * mats
    group_rows = all_rows // GROUPS
    n_queries = query_grads.shape[0] * n_ex
    share = n_queries // n_mat
    dma = pltpu.SemaphoreType.DMA
    in_vmem = pl.BlockSpec(memory_space=pltpu.VMEM)
    anywhere = pl.BlockSpec(memory_space=pl.ANY)
    parts = pl.pallas_call(
        functools.partial(kernel, n_ex, n_mat),
        name="influence",
        out_shape=(
            pltpu.VMEM((mats, rows, columns), BF16),
            pltpu.VMEM((LAST, share, group_rows), F32),
            pltpu.VMEM((2, share, group_rows // 2), F32),
            pltpu.VMEM((LAST, len(Z_PEERS), share, group_rows), BF16),
            pltpu.VMEM((len(PEERS), 2, share, group_rows // 2), BF16),
        ),
        in_specs=[anywhere] * 3,
        out_specs=(in_vmem,) * 5,
        scratch_shapes=[
            pltpu.VMEM((GROUPS, group_rows, columns), BF16),
            pltpu.VMEM((GROUPS, group_rows, columns), BF16),
            pltpu.VMEM((GROUPS, group_rows, columns), BF16),
            pltpu.VMEM((columns, columns), BF16),
            pltpu.VMEM((n_queries, columns), BF16),
            pltpu.VMEM((n_queries, columns), BF16),
            pltpu.VMEM((n_queries, group_rows), F32),
            pltpu.VMEM((LAST, n_queries // 2, group_rows), BF16),
            pltpu.VMEM((LAST, n_queries // 2, group_rows), BF16),
            pltpu.VMEM((LAST, n_queries // 2, group_rows), BF16),
            pltpu.VMEM((2, n_queries, group_rows // 2), BF16),
            pltpu.VMEM((n_queries, group_rows // 2), F32),
            dma((GROUPS,)),
            dma,
            dma,
            dma((GROUPS + 1,)),
            dma((GROUPS + 1,)),
            dma((2,)),
            dma((2,)),
            dma((LAST,)),
            dma((LAST,)),
            dma((LAST,)),
            dma((LAST,)),
            dma,
            dma,
        ],
        compiler_params=pltpu.CompilerParams(
            collective_id=0, has_side_effects=True, vmem_limit_bytes=40 * 2**20
        ),
        cost_estimate=pl.CostEstimate(
            flops=2 * all_rows * columns * (columns + n_queries),
            bytes_accessed=2 * columns * (2 * all_rows + columns),
            transcendentals=0,
        ),
    )(
        in_hbm(train_grads.reshape(all_rows, columns)),
        in_hbm(inverse_hessian.reshape(columns, columns)),
        in_hbm(query_grads.reshape(query_grads.shape[0], columns)),
    )
    pre, scores = pl.pallas_call(
        finish,
        name="write_out",
        out_shape=(
            pltpu.HBM((mats, rows, columns), BF16),
            pltpu.HBM((share, all_rows), F32),
        ),
        in_specs=[in_vmem] * 5,
        out_specs=(anywhere,) * 2,
        scratch_shapes=[pltpu.VMEM((share, all_rows), F32), dma((4,)), dma],
        compiler_params=pltpu.CompilerParams(vmem_limit_bytes=16 * 2**20),
    )(*parts)
    return pre.reshape(all_rows, 1, columns), scores


def solution(mesh):
    return jax.shard_map(
        functools.partial(on_device, mesh.shape["ex"], mesh.shape["mat"]),
        mesh=mesh,
        in_specs=(P(("ex", "mat"), None, None), P("mat", None, None), P("ex", "mat", None)),
        out_specs=(P("ex", "mat", None), P("mat", "ex")),
        check_vma=False,
    )
```
